32 devices in a mesh: lat: 4 (over y, x), lon: 8 (over z, core).
Axes of the slice: x: 2, y: 2, z: 4, core: 2. Of those that a mesh axis runs over, the one named last changes fastest.
Arguments:
- field: bfloat16 [128, 1024, 128], P('lat', 'lon'), may hold values from -60 to 60
- w_first: bfloat16 [3, 3, 128, 128], replicated, may hold values from -0.1875 to 0.1875
- w_down: bfloat16 [3, 3, 128, 256], replicated, may hold values from -0.1875 to 0.1875
- keep_first: int32 [128, 128], replicated, may hold values 0 or 1
- chan_first: int32 [128], replicated, may hold values 0 or 1
- keep_down: int32 [128, 256], replicated, may hold values 0 or 1
- chan_down: int32 [256], replicated, may hold values 0 or 1
- group_ids: int32 [128], replicated, may hold values from 0 to 31, as said below
- norm_gain: float32 [128], replicated, may hold values from 0.1 to 1.9
- norm_bias: float32 [128], replicated, may hold values from -3 to 3
Outputs:
- student_out: bfloat16 [64, 512, 256], P('lat', 'lon')
- grad_first: float32 [1152, 128], P(('lat', 'lon'))
- grad_down: float32 [1152, 256], P(('lat', 'lon'))
The draws below stay inside these ranges and needn't reach their ends.
Inputs may be any that keep to these rules, and one draw needn't show every extreme that they name: `group_ids`: each of the 32 groups holds exactly 4 channels.
All inputs are finite; a program needn't handle non-finite values.
Results may differ from the reference program's by a relative error of at most 0.005.
Values may be sent and summed in bfloat16 or wider, within the bound.
A program may use at most 128 MiB of HBM per device.

```python
import math
import jax
import jax.numpy as jnp
from jax import lax

CHANNELS = 128
OUT_CHANNELS = 256
GROUPS = 32
LAT_CELLS = 128
LON_CELLS = 1024


def draw_field(key, part):
    key = jax.random.fold_in(key, 11)
    key_rough, key_chan = jax.random.split(key)
    lat_pos = jnp.arange(LAT_CELLS, dtype=jnp.float32) / LAT_CELLS
    chan_scale = jnp.exp(jax.random.uniform(key_chan, (CHANNELS,), jnp.float32, 0.0, math.log(3.0)))
    shape_all = (LAT_CELLS, LON_CELLS, CHANNELS)
    rough_part = jax.random.truncated_normal(key_rough, -5.0, 5.0, shape_all, jnp.float32)
    cell_scale = jnp.exp(math.log(10.0) * lat_pos)[:, None] * jnp.ones((LON_CELLS,), jnp.float32)[None, :]
    return (0.3 * rough_part * cell_scale[:, :, None] * chan_scale).astype(jnp.bfloat16)


def draw_group_ids(key, part):
    key = jax.random.fold_in(key, 7)
    order = jax.random.permutation(key, CHANNELS)
    return (order // (CHANNELS // GROUPS)).astype(jnp.int32)


def plant(result, own_key, smallest, high):
    extent = result.shape
    index_at = [jax.random.randint(jax.random.fold_in(own_key, axis), (), 0, extent[axis]) for axis in range(len(extent))]
    result = result.at[tuple(index_at)].set(smallest)
    longest = extent.index(max(extent))
    index_at[longest] = (index_at[longest] + 1) % extent[longest]
    return result.at[tuple(index_at)].set(high)


def normal_values(rng, dims, deviation, reach, kind=jnp.bfloat16):
    result = deviation * jax.random.normal(rng, dims, jnp.float32)
    return jnp.clip(result, min=-reach, max=reach).astype(kind)


def setup_inputs(seed: int = 0) -> dict:
    streams_of = jax.random.split(jax.random.key(seed), 11)
    return {
        "field": draw_field(jax.random.fold_in(streams_of[10], 71), 0),
        "w_first": normal_values(streams_of[1], (3, 3, CHANNELS, CHANNELS), (9 * CHANNELS) ** -0.5, 0.1875),
        "w_down": normal_values(streams_of[2], (3, 3, CHANNELS, OUT_CHANNELS), (9 * CHANNELS) ** -0.5, 0.1875),
        "keep_first": plant((jax.random.randint(streams_of[3], (CHANNELS, CHANNELS), 0, 4) < 3).astype(jnp.int32), jax.random.fold_in(streams_of[3], 1), 0, 1),
        "chan_first": plant((jax.random.randint(streams_of[4], (CHANNELS,), 0, 8) < 7).astype(jnp.int32), jax.random.fold_in(streams_of[4], 1), 0, 1),
        "keep_down": plant((jax.random.randint(streams_of[5], (CHANNELS, OUT_CHANNELS), 0, 4) < 3).astype(jnp.int32), jax.random.fold_in(streams_of[5], 1), 0, 1),
        "chan_down": plant((jax.random.randint(streams_of[6], (OUT_CHANNELS,), 0, 8) < 7).astype(jnp.int32), jax.random.fold_in(streams_of[6], 1), 0, 1),
        "group_ids": draw_group_ids(jax.random.fold_in(streams_of[10], 71), 0),
        "norm_gain": jnp.clip(1.0 + 0.18 * jax.random.normal(streams_of[8], (CHANNELS,), jnp.float32), 0.1, 1.9),
        "norm_bias": normal_values(streams_of[9], (CHANNELS,), 0.5, 3.0, jnp.float32),
    }


LAYOUT = ('NHWC', 'HWIO', 'NHWC')
EPS = 1e-05
LOSS_WEIGHT = 64.0

def conv_same(values, weight):
    padded = jnp.pad(values, ((1, 1), (0, 0), (0, 0)))
    padded = jnp.concatenate([padded[:, -1:], padded, padded[:, :1]], axis=1)
    return lax.conv_general_dilated(padded[None], weight, (1, 1), 'VALID', dimension_numbers=LAYOUT, precision=lax.Precision.HIGHEST)[0]

def conv_half(values, weight):
    padded = jnp.pad(values, ((1, 0), (0, 0), (0, 0)))
    padded = jnp.concatenate([padded[:, -1:], padded], axis=1)
    return lax.conv_general_dilated(padded[None], weight, (2, 2), 'VALID', dimension_numbers=LAYOUT, precision=lax.Precision.HIGHEST)[0]

def group_mean(sums, member, count):
    grouped = jnp.dot(sums, member, precision=lax.Precision.HIGHEST) / count
    return jnp.dot(grouped, member.T, precision=lax.Precision.HIGHEST)

def norm_parts(pre, member, count, norm_gain, norm_bias):
    center = group_mean(lax.optimization_barrier(jnp.sum(pre, axis=(0, 1))), member, count)
    deviate = pre - center
    variance = group_mean(lax.optimization_barrier(jnp.sum(deviate * deviate, axis=(0, 1))), member, count)
    inv_std = lax.rsqrt(variance + EPS)
    normed_hat = deviate * inv_std
    return (normed_hat, normed_hat * norm_gain + norm_bias, inv_std)

def reference(field, w_first, w_down, keep_first, chan_first, keep_down, chan_down, group_ids, norm_gain, norm_bias):
    mask_first = (keep_first * chan_first[None, :]).astype(jnp.float32)
    mask_down = (keep_down * chan_down[None, :]).astype(jnp.float32)
    teacher_first = w_first.astype(jnp.float32)
    teacher_down = w_down.astype(jnp.float32)
    student_first = (w_first * mask_first.astype(jnp.bfloat16)[None, None]).astype(jnp.float32)
    student_down = (w_down * mask_down.astype(jnp.bfloat16)[None, None]).astype(jnp.float32)
    source = field.astype(jnp.float32)
    member = (group_ids[:, None] == jnp.arange(GROUPS)[None, :]).astype(jnp.float32)
    count = float(LAT_CELLS * LON_CELLS * (CHANNELS // GROUPS))
    pre_teacher = conv_same(source, teacher_first)
    pre_student = conv_same(source, student_first)
    hat_teacher, normed_teacher, inv_teacher = norm_parts(pre_teacher, member, count, norm_gain, norm_bias)
    hat_student, normed_student, inv_student = norm_parts(pre_student, member, count, norm_gain, norm_bias)
    hidden_teacher = jax.nn.silu(normed_teacher).astype(jnp.bfloat16).astype(jnp.float32)
    hidden_student = jax.nn.silu(normed_student).astype(jnp.bfloat16).astype(jnp.float32)
    out_teacher = conv_half(hidden_teacher, teacher_down)
    out_student = conv_half(hidden_student, student_down)
    out_total = float(LAT_CELLS // 2 * (LON_CELLS // 2))
    cotangent = (LOSS_WEIGHT / out_total * (out_student - out_teacher)).astype(jnp.bfloat16).astype(jnp.float32)
    unused, pull_down = jax.vjp(conv_half, hidden_student, student_down)
    grad_hidden, grad_weight_down = pull_down(cotangent)
    grad_down = (grad_weight_down * mask_down[None, None]).reshape(9 * CHANNELS, OUT_CHANNELS)
    sigma = jax.nn.sigmoid(normed_student)
    grad_hat = grad_hidden * sigma * (1.0 + normed_student * (1.0 - sigma)) * norm_gain
    first_mom = group_mean(lax.optimization_barrier(jnp.sum(grad_hat, axis=(0, 1))), member, count)
    second_mom = group_mean(lax.optimization_barrier(jnp.sum(grad_hat * hat_student, axis=(0, 1))), member, count)
    grad_pre = (inv_student * (grad_hat - first_mom - hat_student * second_mom)).astype(jnp.bfloat16).astype(jnp.float32)
    unused_two, pull_first = jax.vjp(lambda weight: conv_same(source, weight), student_first)
    grad_weight_first = pull_first(grad_pre)[0]
    grad_first = (grad_weight_first * mask_first[None, None]).reshape(9 * CHANNELS, CHANNELS)
    return (out_student.astype(jnp.bfloat16), grad_first, grad_down)
```

```python
import functools

import jax
import jax.numpy as jnp
from jax import lax
from jax.experimental import pallas as pl
from jax.experimental.pallas import tpu as pltpu
from jax.sharding import PartitionSpec as P

GROUPS = 32
EPS = 1e-05
LOSS_WEIGHT = 64.0
MESH = pl.DeviceIdType.MESH
F32 = jnp.float32
BF16 = jnp.bfloat16
HIGH = lax.Precision.HIGHEST
BLOCK = 8


def dot(a, b):
    return jnp.dot(a, b, preferred_element_type=F32)


def kernel(
    nlat, nlon, chunk, padded,
    field, w_first, w_down, keep_first, chan_first, keep_down, chan_down, group_ids, gain_ref, bias_ref,
    out_ref, gfirst_ref, gdown_ref,
    ext, tmp, taps, pre, hid, hcol, hcol_in, hcorner, cot, ccol, ccol_in, ccorner, ghat, gturn, cturn,
    wf, wd, wt, gf, gd, send_f, send_d, got_f, got_d, stat_a, stat_b,
    own_sem, halo_s, halo_r, hid_s, hid_r, cot_s, cot_r, sa_s, sa_r, sb_s, sb_r, rf_s, rf_r, rd_s, rd_r,
):
    devices = nlat * nlon
    rows, cols, ch = field.shape
    out_ch = w_down.shape[3]
    half, wide = rows // 2, cols // 2
    lat, lon = lax.axis_index("lat"), lax.axis_index("lon")
    me = lat * nlon + lon
    west, east = lax.rem(lon + nlon - 1, nlon), lax.rem(lon + 1, nlon)
    has_up, has_down = lat > 0, lat < nlat - 1

    def place(index):
        return (index // nlon, lax.rem(index, nlon))

    own = pltpu.make_async_copy(field, ext.at[pl.ds(1, rows), pl.ds(16, cols)], own_sem)
    own.start()

    barrier = pltpu.get_barrier_semaphore()

    def greet(k, carry):
        pl.semaphore_signal(barrier, inc=1, device_id=place(lax.rem(me + k, devices)), device_id_type=MESH)
        return carry

    lax.fori_loop(1, devices, greet, 0)
    pl.semaphore_wait(barrier, devices - 1)

    def remote(src, dst, ssem, rsem, target):
        return pltpu.make_async_remote_copy(
            src_ref=src, dst_ref=dst, send_sem=ssem, recv_sem=rsem, device_id=target, device_id_type=MESH
        )

    def guarded(condition, action):
        if condition is None:
            action()
        else:
            pl.when(condition)(action)

    def begin(plans):
        for copy, sends, _ in plans:
            guarded(sends, copy.start)

    def finish_sends(plans):
        for copy, sends, _ in plans:
            guarded(sends, copy.wait_send)

    def finish_receives(plans):
        for copy, _, receives in plans:
            guarded(receives, copy.wait_recv)

    up, down = jnp.maximum(lat - 1, 0), jnp.minimum(lat + 1, nlat - 1)
    left, right, centre = pl.ds(0, 16), pl.ds(cols - 16, 16), pl.ds(16, cols)
    far = pl.ds(16 + cols, 16)
    first, last = pl.ds(0, 1), pl.ds(rows - 1, 1)
    below = pl.ds(rows + 1, 1)

    def halo(i, src, dst, target, sends, receives):
        return (remote(src, dst, halo_s.at[i], halo_r.at[i], target), sends, receives)

    halos = [
        halo(0, field.at[first], ext.at[below, centre], (up, lon), has_up, has_down),
        halo(1, field.at[last], ext.at[first, centre], (down, lon), has_down, has_up),
        halo(2, field.at[:, left], ext.at[pl.ds(1, rows), far], (lat, west), None, None),
        halo(3, field.at[:, right], ext.at[pl.ds(1, rows), left], (lat, east), None, None),
        halo(4, field.at[first, left], ext.at[below, far], (up, west), has_up, has_down),
        halo(5, field.at[first, right], ext.at[below, left], (up, east), has_up, has_down),
        halo(6, field.at[last, left], ext.at[first, far], (down, west), has_down, has_up),
        halo(7, field.at[last, right], ext.at[first, left], (down, east), has_down, has_up),
    ]
    begin(halos)

    @pl.when(jnp.logical_not(has_up))
    def _():
        ext[0] = jnp.zeros(ext.shape[1:], BF16)

    @pl.when(jnp.logical_not(has_down))
    def _():
        ext[rows + 1] = jnp.zeros(ext.shape[1:], BF16)

    mask_first = (keep_first[...] * chan_first[...]).astype(F32)
    mask_down = (keep_down[...] * chan_down[...]).astype(F32)
    for a in range(3):
        wt[a, out_ch:, :ch] = jnp.zeros((out_ch, ch), BF16)
        for b in range(3):
            here = slice(b * ch, (b + 1) * ch)
            wf[a, here, :ch] = w_first[a, b]
            wf[a, here, ch:] = (w_first[a, b].astype(F32) * mask_first).astype(BF16)
            student = w_down[a, b].astype(F32) * mask_down
            wd[0, a, here] = w_down[a, b]
            wd[1, a, here] = student.astype(BF16)
            turned = student.T.astype(BF16)
            if b == 0:
                wt[a, out_ch:, ch:] = turned
            elif b == 1:
                wt[a, :out_ch, :ch] = turned
            else:
                wt[a, :out_ch, ch:] = turned
    ids = jnp.broadcast_to(group_ids[...].astype(F32), (ch, ch))
    member = (ids == ids.T).astype(F32)
    gain, bias = gain_ref[...], bias_ref[...]

    own.wait()
    finish_receives(halos)

    def spread(r, carry):
        for e in range(2):
            tmp[e] = ext[2 * r + e].astype(F32)
            for k in range(4):
                taps[e, r, :, k * ch : (k + 1) * ch] = tmp[e, pl.ds(15 + k, wide, stride=2), :].astype(BF16)
        return carry

    lax.fori_loop(0, half + 1, spread, 0)

    size = BLOCK * wide
    total = jnp.zeros((1, 2 * ch), F32)
    for e in range(2):
        for p in range(2):

            def convolve(step, carry, e=e, p=p):
                r = step * BLOCK
                acc = None
                for a in range(3):
                    lhs = taps[(e + a) % 2, pl.ds(r + (e + a) // 2, BLOCK), :, p * ch : (p + 3) * ch]
                    part = dot(lhs.reshape(size, 3 * ch), wf[a])
                    acc = part if acc is None else acc + part
                pre[e, p, pl.ds(r, BLOCK)] = acc.reshape(BLOCK, wide, 2 * ch)
                return carry + jnp.sum(acc, axis=0, keepdims=True)

            total = lax.fori_loop(0, half // BLOCK, convolve, total)
    finish_sends(halos)

    def fold(value):
        return jnp.concatenate([value[:, :ch], value[:, ch:]], axis=0)

    cells = float(rows * cols)
    mean = total / cells

    def squares(r, carry):
        for e in range(2):
            for p in range(2):
                gap = pre[e, p, r] - mean
                carry = carry + jnp.sum(gap * gap, axis=0, keepdims=True)
        return carry

    spread_sum = lax.fori_loop(0, half, squares, jnp.zeros((1, 2 * ch), F32))

    def everyone(source, target, ssem, rsem):
        def start(k, carry):
            to = lax.rem(me + k, devices)
            remote(source(to), target.at[me], ssem.at[k], rsem.at[k], place(to)).start()
            return carry

        def receive(k, carry):
            at = lax.rem(me + devices - k, devices)
            remote(source(at), target.at[at], ssem.at[k], rsem.at[k], place(at)).wait_recv()
            return carry

        def sent(k, carry):
            to = lax.rem(me + k, devices)
            remote(source(to), target.at[me], ssem.at[k], rsem.at[k], place(to)).wait_send()
            return carry

        return (
            lambda: lax.fori_loop(1, devices, start, 0),
            lambda: lax.fori_loop(1, devices, receive, 0),
            lambda: lax.fori_loop(1, devices, sent, 0),
        )

    def grouped(value):
        return jnp.dot(value, member, precision=HIGH, preferred_element_type=F32)

    per_group = ch // GROUPS
    count = cells * devices * per_group
    stat_a[me] = jnp.concatenate([fold(mean), fold(spread_sum), jnp.zeros((4, ch), F32)], axis=0)
    go, receive, sent_a = everyone(lambda to: stat_a.at[me], stat_a, sa_s, sa_r)
    go()
    receive()
    stats = stat_a[...]
    centre8 = grouped(jnp.sum(stats, axis=0)) / float(devices * per_group)
    centre2 = centre8[0:2]
    drift = stats[:, 0:2] - centre2[None]
    moment = jnp.sum(stats[:, 2:4] + cells * (drift * drift), axis=0)
    variance = grouped(jnp.concatenate([moment, jnp.zeros((6, ch), F32)], axis=0))[0:2] / count
    inv2 = lax.rsqrt(variance + EPS)
    centre_s, inv_s = centre2[1:2], inv2[1:2]
    centre_both = jnp.concatenate([centre2[0:1], centre_s], axis=1)
    inv_both = jnp.concatenate([inv2[0:1], inv_s], axis=1)
    gain_both = jnp.concatenate([gain, gain], axis=1)
    bias_both = jnp.concatenate([bias, bias], axis=1)

    def activate(r, carry):
        for e in range(2):
            at = r + 1 if e else r + half + 1
            for p in range(2):
                normed = (pre[e, p, r] - centre_both) * inv_both * gain_both + bias_both
                value = normed * jax.nn.sigmoid(normed)
                rounded = value.astype(BF16)
                for net in range(2):
                    hid[net, at, :, (p + 1) * ch : (p + 2) * ch] = rounded[:, net * ch : (net + 1) * ch]
                if p:
                    value = rounded.astype(F32)
                    hcol[pl.ds(e * half + r, 1), :] = value[wide - 1 :, :]
                    rolled = pltpu.roll(value, 1, 0).astype(BF16)
                    for net in range(2):
                        hid[net, at, :, :ch] = rolled[:, net * ch : (net + 1) * ch]
        return carry

    lax.fori_loop(0, half, activate, 0)
    hids = [
        (remote(hid.at[:, half], hid.at[:, 0], hid_s.at[0], hid_r.at[0], (down, lon)), has_down, has_up),
        (remote(hcol, hcol_in, hid_s.at[1], hid_r.at[1], (lat, east)), None, None),
        (remote(hcol.at[pl.ds(rows - 8, 8)], hcorner, hid_s.at[2], hid_r.at[2], (down, east)), has_down, has_up),
    ]
    begin(hids)
    sent_a()

    @pl.when(jnp.logical_not(has_up))
    def _():
        hid[:, 0] = jnp.zeros((2, wide, 3 * ch), BF16)
        hcorner[...] = jnp.zeros(hcorner.shape, F32)

    finish_sends(hids)
    finish_receives(hids)
    top = lax.broadcasted_iota(jnp.int32, (16, ch), 0) == 0

    def put_west(at, value):
        for net in range(2):
            tile = hid[net, at, :16, :ch].astype(F32)
            new = jnp.broadcast_to(value[:, net * ch : (net + 1) * ch], (16, ch))
            hid[net, at, :16, :ch] = jnp.where(top, new, tile).astype(BF16)

    def mend(r, carry):
        put_west(r + half + 1, hcol_in[pl.ds(r, 1), :])
        put_west(r + 1, hcol_in[pl.ds(r + half, 1), :])
        return carry

    lax.fori_loop(0, half, mend, 0)
    put_west(0, hcorner[7:8, :])

    starts = (0, half + 1, 1)
    scale = LOSS_WEIGHT / float(half * wide * devices)

    def shrink(step, carry):
        r = step * BLOCK
        both = []
        for net in range(2):
            acc = None
            for a in range(3):
                lhs = hid[net, pl.ds(r + starts[a], BLOCK)].reshape(size, 3 * ch)
                part = dot(lhs, wd[net, a])
                acc = part if acc is None else acc + part
            both.append(acc)
        out_ref[pl.ds(r, BLOCK)] = both[1].astype(BF16).reshape(BLOCK, wide, out_ch)
        ct = (scale * (both[1] - both[0])).astype(BF16)
        cot[pl.ds(r, BLOCK), :, :out_ch] = ct.reshape(BLOCK, wide, out_ch)
        ct32 = ct.astype(F32)
        for q in range(BLOCK):
            line = ct32[q * wide : (q + 1) * wide]
            ccol[pl.ds(r + q, 1), :] = line[0:1]
            cot[r + q, :, out_ch:] = pltpu.roll(line, wide - 1, 0).astype(BF16)
        return carry

    lax.fori_loop(0, half // BLOCK, shrink, 0)
    cots = [
        (remote(cot.at[0], cot.at[half], cot_s.at[0], cot_r.at[0], (up, lon)), has_up, has_down),
        (remote(ccol, ccol_in, cot_s.at[1], cot_r.at[1], (lat, west)), None, None),
        (remote(ccol.at[pl.ds(0, 8)], ccorner, cot_s.at[2], cot_r.at[2], (up, west)), has_up, has_down),
    ]
    begin(cots)

    @pl.when(jnp.logical_not(has_down))
    def _():
        cot[half] = jnp.zeros((wide, 2 * out_ch), BF16)
        ccorner[...] = jnp.zeros(ccorner.shape, F32)

    for step in range(half // BLOCK):
        piece = cot[step * BLOCK : (step + 1) * BLOCK, :, :out_ch].reshape(size, out_ch)
        cturn[:, step * size : (step + 1) * size] = piece.astype(F32).T.astype(BF16)
    finish_sends(cots)
    finish_receives(cots)
    bottom = lax.broadcasted_iota(jnp.int32, (16, out_ch), 0) == 15

    def put_east(at, value):
        tile = cot[at, wide - 16 :, out_ch:].astype(F32)
        cot[at, wide - 16 :, out_ch:] = jnp.where(bottom, jnp.broadcast_to(value, (16, out_ch)), tile).astype(BF16)

    def mend_east(r, carry):
        put_east(r, ccol_in[pl.ds(r, 1), :])
        return carry

    lax.fori_loop(0, half, mend_east, 0)
    put_east(half, ccorner[0:1, :])

    def backward(step, carry):
        r = step * BLOCK
        here = cot[pl.ds(r, BLOCK)].reshape(size, 2 * out_ch)
        after = cot[pl.ds(r + 1, BLOCK)].reshape(size, 2 * out_ch)
        pair = (dot(here, wt[1]), dot(here, wt[2]) + dot(after, wt[0]))
        one, two = carry
        for e in range(2):
            for p in range(2):
                hat = (pre[e, p, pl.ds(r, BLOCK), :, ch:].reshape(size, ch) - centre_s) * inv_s
                normed = hat * gain + bias
                sigma = jax.nn.sigmoid(normed)
                value = pair[e][:, p * ch : (p + 1) * ch] * sigma * (1.0 + normed * (1.0 - sigma)) * gain
                ghat[e, pl.ds(r, BLOCK), :, p * ch : (p + 1) * ch] = value.reshape(BLOCK, wide, ch)
                one = one + jnp.sum(value, axis=0, keepdims=True)
                two = two + jnp.sum(value * hat, axis=0, keepdims=True)
        return one, two

    zero = jnp.zeros((1, ch), F32)
    one, two = lax.fori_loop(0, half // BLOCK, backward, (zero, zero))
    stat_b[me] = jnp.concatenate([one, two, jnp.zeros((6, ch), F32)], axis=0)
    go, receive_b, sent_b = everyone(lambda to: stat_b.at[me], stat_b, sb_s, sb_r)
    go()

    def pack(grads, buffer):
        for d in range(devices):
            buffer[d] = grads[d * chunk : d * chunk + padded, :].astype(BF16)

    gd[9 * ch :, :] = jnp.zeros((16, out_ch), F32)
    gf[9 * ch :, :] = jnp.zeros((16, ch), F32)
    for a in range(3):
        turned = dot(cturn[...], hid[1, starts[a] : starts[a] + half].reshape(half * wide, 3 * ch))
        for b in range(3):
            at = (a * 3 + b) * ch
            gd[at : at + ch, :] = turned[:, b * ch : (b + 1) * ch].T * mask_down
    pack(gd, send_d)
    go_d, receive_d, sent_d = everyone(lambda to: send_d.at[to], got_d, rd_s, rd_r)
    go_d()
    got_d[me] = send_d[me]

    receive_b()
    back = grouped(jnp.sum(stat_b[...], axis=0)) / count
    m1, m2 = back[0:1], back[1:2]
    for e in range(2):
        for step in range(half // BLOCK):
            r = step * BLOCK
            for p in range(2):
                hat = (pre[e, p, r : r + BLOCK, :, ch:].reshape(size, ch) - centre_s) * inv_s
                value = ghat[e, r : r + BLOCK, :, p * ch : (p + 1) * ch].reshape(size, ch)
                gpre = inv_s * (value - m1 - hat * m2)
                gturn[e, p * ch : (p + 1) * ch, step * size : (step + 1) * size] = gpre.T.astype(BF16)
    for a in range(3):
        acc = None
        for e in range(2):
            start = (e + a) // 2
            part = dot(gturn[e], taps[(e + a) % 2, start : start + half].reshape(half * wide, 4 * ch))
            acc = part if acc is None else acc + part
        for b in range(3):
            at = (a * 3 + b) * ch
            block = acc[:ch, b * ch : (b + 1) * ch] + acc[ch:, (b + 1) * ch : (b + 2) * ch]
            gf[at : at + ch, :] = block.T * mask_first
    pack(gf, send_f)
    go_f, receive_f, sent_f = everyone(lambda to: send_f.at[to], got_f, rf_s, rf_r)
    go_f()
    got_f[me] = send_f[me]

    def add_up(got, width):
        def add(d, acc):
            return acc + got[d].astype(F32)

        return lax.fori_loop(0, devices, add, jnp.zeros((padded, width), F32))[:chunk]

    receive_d()
    gdown_ref[...] = add_up(got_d, out_ch)
    receive_f()
    gfirst_ref[...] = add_up(got_f, ch)
    sent_b()
    sent_d()
    sent_f()


def local(nlat, nlon, field, w_first, w_down, keep_first, chan_first, keep_down, chan_down, group_ids, norm_gain, norm_bias):
    rows, cols, ch = field.shape
    out_ch = w_down.shape[3]
    devices = nlat * nlon
    half, wide = rows // 2, cols // 2
    chunk = 9 * ch // devices
    padded = -(-chunk // 16) * 16
    vmem = pl.BlockSpec(memory_space=pltpu.VMEM)
    dma = pltpu.SemaphoreType.DMA
    S = pltpu.VMEM
    return tuple(
        pl.pallas_call(
            functools.partial(kernel, nlat, nlon, chunk, padded),
            out_shape=(
                jax.ShapeDtypeStruct((half, wide, out_ch), BF16),
                jax.ShapeDtypeStruct((chunk, ch), F32),
                jax.ShapeDtypeStruct((chunk, out_ch), F32),
            ),
            in_specs=[pl.BlockSpec(memory_space=pl.ANY)] + [vmem] * 9,
            out_specs=(vmem, vmem, vmem),
            scratch_shapes=[
                S((rows + 2, cols + 32, ch), BF16),
                S((2, cols + 32, ch), F32),
                S((2, half + 1, wide, 4 * ch), BF16),
                S((2, 2, half, wide, 2 * ch), F32),
                S((2, rows + 1, wide, 3 * ch), BF16),
                S((rows, 2 * ch), F32),
                S((rows, 2 * ch), F32),
                S((8, 2 * ch), F32),
                S((half + 1, wide, 2 * out_ch), BF16),
                S((half, out_ch), F32),
                S((half, out_ch), F32),
                S((8, out_ch), F32),
                S((2, half, wide, 2 * ch), F32),
                S((2, 2 * ch, half * wide), BF16),
                S((out_ch, half * wide), BF16),
                S((3, 3 * ch, 2 * ch), BF16),
                S((2, 3, 3 * ch, out_ch), BF16),
                S((3, 2 * out_ch, 2 * ch), BF16),
                S((9 * ch + 16, ch), F32),
                S((9 * ch + 16, out_ch), F32),
                S((devices, padded, ch), BF16),
                S((devices, padded, out_ch), BF16),
                S((devices, padded, ch), BF16),
                S((devices, padded, out_ch), BF16),
                S((devices, 8, ch), F32),
                S((devices, 8, ch), F32),
                dma,
                dma((8,)), dma((8,)),
                dma((3,)), dma((3,)),
                dma((3,)), dma((3,)),
                dma((devices,)), dma((devices,)),
                dma((devices,)), dma((devices,)),
                dma((devices,)), dma((devices,)),
                dma((devices,)), dma((devices,)),
            ],
            compiler_params=pltpu.CompilerParams(
                collective_id=0, has_side_effects=True, vmem_limit_bytes=56 * 1024 * 1024
            ),
        )(
            field,
            w_first,
            w_down,
            keep_first,
            chan_first.reshape(1, ch),
            keep_down,
            chan_down.reshape(1, out_ch),
            group_ids.reshape(1, ch),
            norm_gain.reshape(1, ch),
            norm_bias.reshape(1, ch),
        )
    )


def solution(mesh):
    return jax.shard_map(
        functools.partial(local, mesh.shape["lat"], mesh.shape["lon"]),
        mesh=mesh,
        in_specs=(P("lat", "lon", None), P(), P(), P(), P(), P(), P(), P(), P(), P()),
        out_specs=(P("lat", "lon", None), P(("lat", "lon"), None), P(("lat", "lon"), None)),
        check_vma=False,
    )
```

```python
import functools

import jax
import jax.numpy as jnp
from jax import lax
from jax.experimental import pallas as pl
from jax.experimental.pallas import tpu as pltpu
from jax.sharding import PartitionSpec as P

GROUPS = 32
EPS = 1e-05
LOSS_WEIGHT = 64.0
MESH = pl.DeviceIdType.MESH
F32 = jnp.float32
BF16 = jnp.bfloat16
HIGH = lax.Precision.HIGHEST
BLOCK = 8


def dot(a, b):
    return jnp.dot(a, b, preferred_element_type=F32)


def kernel(
    nlat, nlon, chunk, padded,
    field, w_first, w_down, keep_first, chan_first, keep_down, chan_down, group_ids, gain_ref, bias_ref,
    out_ref, gfirst_ref, gdown_ref,
    ext, tmp, taps, pre, hid, hcol, hcol_in, hcorner, cot, ccol, ccol_in, ccorner, ghat, gturn, cturn,
    wf, wd, wt, gf, gd, send_f, send_d, other_f, other_d, merged_f, merged_d, got_f, got_d, stat_a, stat_b,
    own_sem, halo_s, halo_r, hid_s, hid_r, cot_s, cot_r, sa_s, sa_r, sb_s, sb_r, swap_s, swap_r, rf_s, rf_r, rd_s, rd_r,
):
    devices = nlat * nlon
    rows, cols, ch = field.shape
    out_ch = w_down.shape[3]
    half, wide = rows // 2, cols // 2
    lat, lon = lax.axis_index("lat"), lax.axis_index("lon")
    me = lat * nlon + lon
    west, east = lax.rem(lon + nlon - 1, nlon), lax.rem(lon + 1, nlon)
    has_up, has_down = lat > 0, lat < nlat - 1

    def place(index):
        return (index // nlon, lax.rem(index, nlon))

    own = pltpu.make_async_copy(field, ext.at[pl.ds(1, rows), pl.ds(16, cols)], own_sem)
    own.start()

    barrier = pltpu.get_barrier_semaphore()

    def greet(k, carry):
        pl.semaphore_signal(barrier, inc=1, device_id=place(lax.rem(me + k, devices)), device_id_type=MESH)
        return carry

    lax.fori_loop(1, devices, greet, 0)
    pl.semaphore_wait(barrier, devices - 1)

    def remote(src, dst, ssem, rsem, target):
        return pltpu.make_async_remote_copy(
            src_ref=src, dst_ref=dst, send_sem=ssem, recv_sem=rsem, device_id=target, device_id_type=MESH
        )

    def guarded(condition, action):
        if condition is None:
            action()
        else:
            pl.when(condition)(action)

    def begin(plans):
        for copy, sends, _ in plans:
            guarded(sends, copy.start)

    def finish_sends(plans):
        for copy, sends, _ in plans:
            guarded(sends, copy.wait_send)

    def finish_receives(plans):
        for copy, _, receives in plans:
            guarded(receives, copy.wait_recv)

    up, down = jnp.maximum(lat - 1, 0), jnp.minimum(lat + 1, nlat - 1)
    left, right, centre = pl.ds(0, 16), pl.ds(cols - 16, 16), pl.ds(16, cols)
    far = pl.ds(16 + cols, 16)
    first, last = pl.ds(0, 1), pl.ds(rows - 1, 1)
    below = pl.ds(rows + 1, 1)

    def halo(i, src, dst, target, sends, receives):
        return (remote(src, dst, halo_s.at[i], halo_r.at[i], target), sends, receives)

    halos = [
        halo(0, field.at[first], ext.at[below, centre], (up, lon), has_up, has_down),
        halo(1, field.at[last], ext.at[first, centre], (down, lon), has_down, has_up),
        halo(2, field.at[:, left], ext.at[pl.ds(1, rows), far], (lat, west), None, None),
        halo(3, field.at[:, right], ext.at[pl.ds(1, rows), left], (lat, east), None, None),
        halo(4, field.at[first, left], ext.at[below, far], (up, west), has_up, has_down),
        halo(5, field.at[first, right], ext.at[below, left], (up, east), has_up, has_down),
        halo(6, field.at[last, left], ext.at[first, far], (down, west), has_down, has_up),
        halo(7, field.at[last, right], ext.at[first, left], (down, east), has_down, has_up),
    ]
    begin(halos)

    @pl.when(jnp.logical_not(has_up))
    def _():
        ext[0] = jnp.zeros(ext.shape[1:], BF16)

    @pl.when(jnp.logical_not(has_down))
    def _():
        ext[rows + 1] = jnp.zeros(ext.shape[1:], BF16)

    mask_first = (keep_first[...] * chan_first[...]).astype(F32)
    mask_down = (keep_down[...] * chan_down[...]).astype(F32)
    for a in range(3):
        wt[a, out_ch:, :ch] = jnp.zeros((out_ch, ch), BF16)
        for b in range(3):
            here = slice(b * ch, (b + 1) * ch)
            wf[a, here, :ch] = w_first[a, b]
            wf[a, here, ch:] = (w_first[a, b].astype(F32) * mask_first).astype(BF16)
            student = w_down[a, b].astype(F32) * mask_down
            wd[0, a, here] = w_down[a, b]
            wd[1, a, here] = student.astype(BF16)
            turned = student.T.astype(BF16)
            if b == 0:
                wt[a, out_ch:, ch:] = turned
            elif b == 1:
                wt[a, :out_ch, :ch] = turned
            else:
                wt[a, :out_ch, ch:] = turned
    ids = jnp.broadcast_to(group_ids[...].astype(F32), (ch, ch))
    member = (ids == ids.T).astype(F32)
    gain, bias = gain_ref[...], bias_ref[...]

    own.wait()
    finish_receives(halos)

    def spread(r, carry):
        for e in range(2):
            tmp[e] = ext[2 * r + e].astype(F32)
            for k in range(4):
                taps[e, r, :, k * ch : (k + 1) * ch] = tmp[e, pl.ds(15 + k, wide, stride=2), :].astype(BF16)
        return carry

    lax.fori_loop(0, half + 1, spread, 0)

    size = BLOCK * wide
    total = jnp.zeros((1, 2 * ch), F32)
    for e in range(2):
        for p in range(2):

            def convolve(step, carry, e=e, p=p):
                r = step * BLOCK
                acc = None
                for a in range(3):
                    lhs = taps[(e + a) % 2, pl.ds(r + (e + a) // 2, BLOCK), :, p * ch : (p + 3) * ch]
                    part = dot(lhs.reshape(size, 3 * ch), wf[a])
                    acc = part if acc is None else acc + part
                pre[e, p, pl.ds(r, BLOCK)] = acc.reshape(BLOCK, wide, 2 * ch)
                return carry + jnp.sum(acc, axis=0, keepdims=True)

            total = lax.fori_loop(0, half // BLOCK, convolve, total)
    finish_sends(halos)

    def fold(value):
        return jnp.concatenate([value[:, :ch], value[:, ch:]], axis=0)

    cells = float(rows * cols)
    mean = total / cells

    def squares(r, carry):
        for e in range(2):
            for p in range(2):
                gap = pre[e, p, r] - mean
                carry = carry + jnp.sum(gap * gap, axis=0, keepdims=True)
        return carry

    spread_sum = lax.fori_loop(0, half, squares, jnp.zeros((1, 2 * ch), F32))

    def everyone(source, target, ssem, rsem):
        def start(k, carry):
            to = lax.rem(me + k, devices)
            remote(source(to), target.at[me], ssem.at[k], rsem.at[k], place(to)).start()
            return carry

        def receive(k, carry):
            at = lax.rem(me + devices - k, devices)
            remote(source(at), target.at[at], ssem.at[k], rsem.at[k], place(at)).wait_recv()
            return carry

        def sent(k, carry):
            to = lax.rem(me + k, devices)
            remote(source(to), target.at[me], ssem.at[k], rsem.at[k], place(to)).wait_send()
            return carry

        return (
            lambda: lax.fori_loop(1, devices, start, 0),
            lambda: lax.fori_loop(1, devices, receive, 0),
            lambda: lax.fori_loop(1, devices, sent, 0),
        )

    def grouped(value):
        return jnp.dot(value, member, precision=HIGH, preferred_element_type=F32)

    per_group = ch // GROUPS
    count = cells * devices * per_group
    stat_a[me] = jnp.concatenate([fold(mean), fold(spread_sum), jnp.zeros((4, ch), F32)], axis=0)
    go, receive, sent_a = everyone(lambda to: stat_a.at[me], stat_a, sa_s, sa_r)
    go()
    receive()
    stats = stat_a[...]
    centre8 = grouped(jnp.sum(stats, axis=0)) / float(devices * per_group)
    centre2 = centre8[0:2]
    drift = stats[:, 0:2] - centre2[None]
    moment = jnp.sum(stats[:, 2:4] + cells * (drift * drift), axis=0)
    variance = grouped(jnp.concatenate([moment, jnp.zeros((6, ch), F32)], axis=0))[0:2] / count
    inv2 = lax.rsqrt(variance + EPS)
    centre_s, inv_s = centre2[1:2], inv2[1:2]
    centre_both = jnp.concatenate([centre2[0:1], centre_s], axis=1)
    inv_both = jnp.concatenate([inv2[0:1], inv_s], axis=1)
    gain_both = jnp.concatenate([gain, gain], axis=1)
    bias_both = jnp.concatenate([bias, bias], axis=1)

    def activate(r, carry):
        for e in range(2):
            at = r + 1 if e else r + half + 1
            for p in range(2):
                normed = (pre[e, p, r] - centre_both) * inv_both * gain_both + bias_both
                value = normed * jax.nn.sigmoid(normed)
                rounded = value.astype(BF16)
                for net in range(2):
                    hid[net, at, :, (p + 1) * ch : (p + 2) * ch] = rounded[:, net * ch : (net + 1) * ch]
                if p:
                    value = rounded.astype(F32)
                    hcol[pl.ds(e * half + r, 1), :] = value[wide - 1 :, :]
                    rolled = pltpu.roll(value, 1, 0).astype(BF16)
                    for net in range(2):
                        hid[net, at, :, :ch] = rolled[:, net * ch : (net + 1) * ch]
        return carry

    lax.fori_loop(0, half, activate, 0)
    hids = [
        (remote(hid.at[:, half], hid.at[:, 0], hid_s.at[0], hid_r.at[0], (down, lon)), has_down, has_up),
        (remote(hcol, hcol_in, hid_s.at[1], hid_r.at[1], (lat, east)), None, None),
        (remote(hcol.at[pl.ds(rows - 8, 8)], hcorner, hid_s.at[2], hid_r.at[2], (down, east)), has_down, has_up),
    ]
    begin(hids)
    sent_a()

    @pl.when(jnp.logical_not(has_up))
    def _():
        hid[:, 0] = jnp.zeros((2, wide, 3 * ch), BF16)
        hcorner[...] = jnp.zeros(hcorner.shape, F32)

    finish_sends(hids)
    finish_receives(hids)
    top = lax.broadcasted_iota(jnp.int32, (16, ch), 0) == 0

    def put_west(at, value):
        for net in range(2):
            tile = hid[net, at, :16, :ch].astype(F32)
            new = jnp.broadcast_to(value[:, net * ch : (net + 1) * ch], (16, ch))
            hid[net, at, :16, :ch] = jnp.where(top, new, tile).astype(BF16)

    def mend(r, carry):
        put_west(r + half + 1, hcol_in[pl.ds(r, 1), :])
        put_west(r + 1, hcol_in[pl.ds(r + half, 1), :])
        return carry

    lax.fori_loop(0, half, mend, 0)
    put_west(0, hcorner[7:8, :])

    starts = (0, half + 1, 1)
    scale = LOSS_WEIGHT / float(half * wide * devices)

    def shrink(step, carry):
        r = step * BLOCK
        both = []
        for net in range(2):
            acc = None
            for a in range(3):
                lhs = hid[net, pl.ds(r + starts[a], BLOCK)].reshape(size, 3 * ch)
                part = dot(lhs, wd[net, a])
                acc = part if acc is None else acc + part
            both.append(acc)
        out_ref[pl.ds(r, BLOCK)] = both[1].astype(BF16).reshape(BLOCK, wide, out_ch)
        ct = (scale * (both[1] - both[0])).astype(BF16)
        cot[pl.ds(r, BLOCK), :, :out_ch] = ct.reshape(BLOCK, wide, out_ch)
        ct32 = ct.astype(F32)
        for q in range(BLOCK):
            line = ct32[q * wide : (q + 1) * wide]
            ccol[pl.ds(r + q, 1), :] = line[0:1]
            cot[r + q, :, out_ch:] = pltpu.roll(line, wide - 1, 0).astype(BF16)
        return carry

    lax.fori_loop(0, half // BLOCK, shrink, 0)
    cots = [
        (remote(cot.at[0], cot.at[half], cot_s.at[0], cot_r.at[0], (up, lon)), has_up, has_down),
        (remote(ccol, ccol_in, cot_s.at[1], cot_r.at[1], (lat, west)), None, None),
        (remote(ccol.at[pl.ds(0, 8)], ccorner, cot_s.at[2], cot_r.at[2], (up, west)), has_up, has_down),
    ]
    begin(cots)

    @pl.when(jnp.logical_not(has_down))
    def _():
        cot[half] = jnp.zeros((wide, 2 * out_ch), BF16)
        ccorner[...] = jnp.zeros(ccorner.shape, F32)

    for step in range(half // BLOCK):
        piece = cot[step * BLOCK : (step + 1) * BLOCK, :, :out_ch].reshape(size, out_ch)
        cturn[:, step * size : (step + 1) * size] = piece.astype(F32).T.astype(BF16)
    finish_sends(cots)
    finish_receives(cots)
    bottom = lax.broadcasted_iota(jnp.int32, (16, out_ch), 0) == 15

    def put_east(at, value):
        tile = cot[at, wide - 16 :, out_ch:].astype(F32)
        cot[at, wide - 16 :, out_ch:] = jnp.where(bottom, jnp.broadcast_to(value, (16, out_ch)), tile).astype(BF16)

    def mend_east(r, carry):
        put_east(r, ccol_in[pl.ds(r, 1), :])
        return carry

    lax.fori_loop(0, half, mend_east, 0)
    put_east(half, ccorner[0:1, :])

    def backward(step, carry):
        r = step * BLOCK
        here = cot[pl.ds(r, BLOCK)].reshape(size, 2 * out_ch)
        after = cot[pl.ds(r + 1, BLOCK)].reshape(size, 2 * out_ch)
        pair = (dot(here, wt[1]), dot(here, wt[2]) + dot(after, wt[0]))
        one, two = carry
        for e in range(2):
            for p in range(2):
                hat = (pre[e, p, pl.ds(r, BLOCK), :, ch:].reshape(size, ch) - centre_s) * inv_s
                normed = hat * gain + bias
                sigma = jax.nn.sigmoid(normed)
                value = pair[e][:, p * ch : (p + 1) * ch] * sigma * (1.0 + normed * (1.0 - sigma)) * gain
                ghat[e, pl.ds(r, BLOCK), :, p * ch : (p + 1) * ch] = value.reshape(BLOCK, wide, ch)
                one = one + jnp.sum(value, axis=0, keepdims=True)
                two = two + jnp.sum(value * hat, axis=0, keepdims=True)
        return one, two

    zero = jnp.zeros((1, ch), F32)
    one, two = lax.fori_loop(0, half // BLOCK, backward, (zero, zero))
    stat_b[me] = jnp.concatenate([one, two, jnp.zeros((6, ch), F32)], axis=0)
    go, receive_b, sent_b = everyone(lambda to: stat_b.at[me], stat_b, sb_s, sb_r)
    go()

    pairs = devices // 2
    core = lax.rem(lon, 2)
    mine = me // 2
    mate = (lat, lon + 1 - 2 * core)

    def pack(grads, buffer):
        for d in range(devices):
            buffer[d % 2, d // 2] = grads[d * chunk : d * chunk + padded, :].astype(BF16)

    def merge(buffer, other, merged, got):
        def one_chunk(h, carry):
            merged[h] = (buffer[core, h].astype(F32) + other[h].astype(F32)).astype(BF16)
            return carry

        lax.fori_loop(0, pairs, one_chunk, 0)
        got[mine] = merged[mine]

    def scatter(merged, got, ssem, rsem):
        def owner(h):
            return place(2 * h + core)

        def start(k, carry):
            to = lax.rem(mine + k, pairs)
            remote(merged.at[to], got.at[mine], ssem.at[k], rsem.at[k], owner(to)).start()
            return carry

        def receive(k, carry):
            at = lax.rem(mine + pairs - k, pairs)
            remote(merged.at[at], got.at[at], ssem.at[k], rsem.at[k], owner(at)).wait_recv()
            return carry

        def sent(k, carry):
            to = lax.rem(mine + k, pairs)
            remote(merged.at[to], got.at[mine], ssem.at[k], rsem.at[k], owner(to)).wait_send()
            return carry

        return (
            lambda: lax.fori_loop(1, pairs, start, 0),
            lambda: lax.fori_loop(1, pairs, receive, 0),
            lambda: lax.fori_loop(1, pairs, sent, 0),
        )

    gd[9 * ch :, :] = jnp.zeros((16, out_ch), F32)
    gf[9 * ch :, :] = jnp.zeros((16, ch), F32)
    for a in range(3):
        turned = dot(cturn[...], hid[1, starts[a] : starts[a] + half].reshape(half * wide, 3 * ch))
        for b in range(3):
            at = (a * 3 + b) * ch
            gd[at : at + ch, :] = turned[:, b * ch : (b + 1) * ch].T * mask_down
    pack(gd, send_d)
    swap_d = remote(send_d.at[1 - core], other_d, swap_s.at[0], swap_r.at[0], mate)
    swap_d.start()
    go_d, receive_d, sent_d = scatter(merged_d, got_d, rd_s, rd_r)

    receive_b()
    back = grouped(jnp.sum(stat_b[...], axis=0)) / count
    m1, m2 = back[0:1], back[1:2]
    for e in range(2):
        for step in range(half // BLOCK):
            r = step * BLOCK
            for p in range(2):
                hat = (pre[e, p, r : r + BLOCK, :, ch:].reshape(size, ch) - centre_s) * inv_s
                value = ghat[e, r : r + BLOCK, :, p * ch : (p + 1) * ch].reshape(size, ch)
                gpre = inv_s * (value - m1 - hat * m2)
                gturn[e, p * ch : (p + 1) * ch, step * size : (step + 1) * size] = gpre.T.astype(BF16)
    swap_d.wait_recv()
    merge(send_d, other_d, merged_d, got_d)
    go_d()
    for a in range(3):
        acc = None
        for e in range(2):
            start = (e + a) // 2
            part = dot(gturn[e], taps[(e + a) % 2, start : start + half].reshape(half * wide, 4 * ch))
            acc = part if acc is None else acc + part
        for b in range(3):
            at = (a * 3 + b) * ch
            block = acc[:ch, b * ch : (b + 1) * ch] + acc[ch:, (b + 1) * ch : (b + 2) * ch]
            gf[at : at + ch, :] = block.T * mask_first
    pack(gf, send_f)
    swap_f = remote(send_f.at[1 - core], other_f, swap_s.at[1], swap_r.at[1], mate)
    swap_f.start()
    go_f, receive_f, sent_f = scatter(merged_f, got_f, rf_s, rf_r)

    def add_up(got, width):
        def add(d, acc):
            return acc + got[d].astype(F32)

        return lax.fori_loop(0, pairs, add, jnp.zeros((padded, width), F32))[:chunk]

    swap_f.wait_recv()
    merge(send_f, other_f, merged_f, got_f)
    go_f()
    receive_d()
    gdown_ref[...] = add_up(got_d, out_ch)
    receive_f()
    gfirst_ref[...] = add_up(got_f, ch)
    sent_b()
    sent_d()
    sent_f()
    swap_d.wait_send()
    swap_f.wait_send()


def local(nlat, nlon, field, w_first, w_down, keep_first, chan_first, keep_down, chan_down, group_ids, norm_gain, norm_bias):
    rows, cols, ch = field.shape
    out_ch = w_down.shape[3]
    devices = nlat * nlon
    pairs = devices // 2
    half, wide = rows // 2, cols // 2
    chunk = 9 * ch // devices
    padded = -(-chunk // 16) * 16
    vmem = pl.BlockSpec(memory_space=pltpu.VMEM)
    dma = pltpu.SemaphoreType.DMA
    S = pltpu.VMEM
    return tuple(
        pl.pallas_call(
            functools.partial(kernel, nlat, nlon, chunk, padded),
            out_shape=(
                jax.ShapeDtypeStruct((half, wide, out_ch), BF16),
                jax.ShapeDtypeStruct((chunk, ch), F32),
                jax.ShapeDtypeStruct((chunk, out_ch), F32),
            ),
            in_specs=[pl.BlockSpec(memory_space=pl.ANY)] + [vmem] * 9,
            out_specs=(vmem, vmem, vmem),
            scratch_shapes=[
                S((rows + 2, cols + 32, ch), BF16),
                S((2, cols + 32, ch), F32),
                S((2, half + 1, wide, 4 * ch), BF16),
                S((2, 2, half, wide, 2 * ch), F32),
                S((2, rows + 1, wide, 3 * ch), BF16),
                S((rows, 2 * ch), F32),
                S((rows, 2 * ch), F32),
                S((8, 2 * ch), F32),
                S((half + 1, wide, 2 * out_ch), BF16),
                S((half, out_ch), F32),
                S((half, out_ch), F32),
                S((8, out_ch), F32),
                S((2, half, wide, 2 * ch), F32),
                S((2, 2 * ch, half * wide), BF16),
                S((out_ch, half * wide), BF16),
                S((3, 3 * ch, 2 * ch), BF16),
                S((2, 3, 3 * ch, out_ch), BF16),
                S((3, 2 * out_ch, 2 * ch), BF16),
                S((9 * ch + 16, ch), F32),
                S((9 * ch + 16, out_ch), F32),
                S((2, pairs, padded, ch), BF16),
                S((2, pairs, padded, out_ch), BF16),
                S((pairs, padded, ch), BF16),
                S((pairs, padded, out_ch), BF16),
                S((pairs, padded, ch), BF16),
                S((pairs, padded, out_ch), BF16),
                S((pairs, padded, ch), BF16),
                S((pairs, padded, out_ch), BF16),
                S((devices, 8, ch), F32),
                S((devices, 8, ch), F32),
                dma,
                dma((8,)), dma((8,)),
                dma((3,)), dma((3,)),
                dma((3,)), dma((3,)),
                dma((devices,)), dma((devices,)),
                dma((devices,)), dma((devices,)),
                dma((2,)), dma((2,)),
                dma((pairs,)), dma((pairs,)),
                dma((pairs,)), dma((pairs,)),
            ],
            compiler_params=pltpu.CompilerParams(
                collective_id=0, has_side_effects=True, vmem_limit_bytes=56 * 1024 * 1024
            ),
        )(
            field,
            w_first,
            w_down,
            keep_first,
            chan_first.reshape(1, ch),
            keep_down,
            chan_down.reshape(1, out_ch),
            group_ids.reshape(1, ch),
            norm_gain.reshape(1, ch),
            norm_bias.reshape(1, ch),
        )
    )


def solution(mesh):
    return jax.shard_map(
        functools.partial(local, mesh.shape["lat"], mesh.shape["lon"]),
        mesh=mesh,
        in_specs=(P("lat", "lon", None), P(), P(), P(), P(), P(), P(), P(), P(), P()),
        out_specs=(P("lat", "lon", None), P(("lat", "lon"), None), P(("lat", "lon"), None)),
        check_vma=False,
    )
```

```python
import functools

import jax
import jax.numpy as jnp
from jax import lax
from jax.experimental import pallas as pl
from jax.experimental.pallas import tpu as pltpu
from jax.sharding import PartitionSpec as P

GROUPS = 32
EPS = 1e-05
LOSS_WEIGHT = 64.0
MESH = pl.DeviceIdType.MESH
F32 = jnp.float32
BF16 = jnp.bfloat16
HIGH = lax.Precision.HIGHEST
BLOCK = 8


def dot(a, b):
    return jnp.dot(a, b, preferred_element_type=F32)


def kernel(
    nlat, nlon, chunk, padded,
    field, w_first, w_down, keep_first, chan_first, keep_down, chan_down, group_ids, gain_ref, bias_ref,
    out_ref, gfirst_ref, gdown_ref,
    ext, tmp, taps, pre, hid, hcol, hcol_in, hcorner, hrow_in, outs, edge, cot, ccol, ccol_in, ccorner, ghat, gturn, cturn,
    wf, wd, wt, gf, gd, send_f, send_d, other_f, other_d, merged_f, merged_d, got_f, got_d, stat_a, stat_b,
    own_sem, halo_s, halo_r, hid_s, hid_r, cot_s, cot_r, sa_s, sa_r, sb_s, sb_r, swap_s, swap_r, rf_s, rf_r, rd_s, rd_r,
):
    devices = nlat * nlon
    rows, cols, ch = field.shape
    out_ch = w_down.shape[3]
    half, wide = rows // 2, cols // 2
    lat, lon = lax.axis_index("lat"), lax.axis_index("lon")
    me = lat * nlon + lon
    west, east = lax.rem(lon + nlon - 1, nlon), lax.rem(lon + 1, nlon)
    has_up, has_down = lat > 0, lat < nlat - 1

    def place(index):
        return (index // nlon, lax.rem(index, nlon))

    own = pltpu.make_async_copy(field, ext.at[pl.ds(1, rows), pl.ds(16, cols)], own_sem)
    own.start()

    barrier = pltpu.get_barrier_semaphore()

    def greet(k, carry):
        pl.semaphore_signal(barrier, inc=1, device_id=place(lax.rem(me + k, devices)), device_id_type=MESH)
        return carry

    lax.fori_loop(1, devices, greet, 0)
    pl.semaphore_wait(barrier, devices - 1)

    def remote(src, dst, ssem, rsem, target):
        return pltpu.make_async_remote_copy(
            src_ref=src, dst_ref=dst, send_sem=ssem, recv_sem=rsem, device_id=target, device_id_type=MESH
        )

    def guarded(condition, action):
        if condition is None:
            action()
        else:
            pl.when(condition)(action)

    def begin(plans):
        for copy, sends, _ in plans:
            guarded(sends, copy.start)

    def finish_sends(plans):
        for copy, sends, _ in plans:
            guarded(sends, copy.wait_send)

    def finish_receives(plans):
        for copy, _, receives in plans:
            guarded(receives, copy.wait_recv)

    up, down = jnp.maximum(lat - 1, 0), jnp.minimum(lat + 1, nlat - 1)
    left, right, centre = pl.ds(0, 16), pl.ds(cols - 16, 16), pl.ds(16, cols)
    far = pl.ds(16 + cols, 16)
    first, last = pl.ds(0, 1), pl.ds(rows - 1, 1)
    below = pl.ds(rows + 1, 1)

    def halo(i, src, dst, target, sends, receives):
        return (remote(src, dst, halo_s.at[i], halo_r.at[i], target), sends, receives)

    halos = [
        halo(0, field.at[first], ext.at[below, centre], (up, lon), has_up, has_down),
        halo(1, field.at[last], ext.at[first, centre], (down, lon), has_down, has_up),
        halo(2, field.at[:, left], ext.at[pl.ds(1, rows), far], (lat, west), None, None),
        halo(3, field.at[:, right], ext.at[pl.ds(1, rows), left], (lat, east), None, None),
        halo(4, field.at[first, left], ext.at[below, far], (up, west), has_up, has_down),
        halo(5, field.at[first, right], ext.at[below, left], (up, east), has_up, has_down),
        halo(6, field.at[last, left], ext.at[first, far], (down, west), has_down, has_up),
        halo(7, field.at[last, right], ext.at[first, left], (down, east), has_down, has_up),
    ]
    begin(halos)

    @pl.when(jnp.logical_not(has_up))
    def _():
        ext[0] = jnp.zeros(ext.shape[1:], BF16)

    @pl.when(jnp.logical_not(has_down))
    def _():
        ext[rows + 1] = jnp.zeros(ext.shape[1:], BF16)

    mask_first = (keep_first[...] * chan_first[...]).astype(F32)
    mask_down = (keep_down[...] * chan_down[...]).astype(F32)
    for a in range(3):
        wt[a, out_ch:, :ch] = jnp.zeros((out_ch, ch), BF16)
        for b in range(3):
            here = slice(b * ch, (b + 1) * ch)
            wf[a, here, :ch] = w_first[a, b]
            wf[a, here, ch:] = (w_first[a, b].astype(F32) * mask_first).astype(BF16)
            student = w_down[a, b].astype(F32) * mask_down
            wd[0, a, here] = w_down[a, b]
            wd[1, a, here] = student.astype(BF16)
            turned = student.T.astype(BF16)
            if b == 0:
                wt[a, out_ch:, ch:] = turned
            elif b == 1:
                wt[a, :out_ch, :ch] = turned
            else:
                wt[a, :out_ch, ch:] = turned
    ids = jnp.broadcast_to(group_ids[...].astype(F32), (ch, ch))
    member = (ids == ids.T).astype(F32)
    gain, bias = gain_ref[...], bias_ref[...]

    top = lax.broadcasted_iota(jnp.int32, (16, ch), 0) == 0
    foot = lax.broadcasted_iota(jnp.int32, (16, ch), 0) == 15
    tmp[...] = jnp.zeros(tmp.shape, F32)

    def spread_row(e, r, at):
        tmp[e, 16 : 16 + cols] = ext[at, 16 : 16 + cols].astype(F32)
        for k in range(4):
            taps[e, r, :, k * ch : (k + 1) * ch] = tmp[e, pl.ds(15 + k, wide, stride=2), :].astype(BF16)

    def mend_row(e, r, at):
        before = pltpu.roll(ext[at, :16].astype(F32), 1, 0)
        after = pltpu.roll(ext[at, 16 + cols :].astype(F32), 15, 0)
        head = taps[e, r, :16, :ch].astype(F32)
        tail = taps[e, r, wide - 16 :, 3 * ch :].astype(F32)
        taps[e, r, :16, :ch] = jnp.where(top, before, head).astype(BF16)
        taps[e, r, wide - 16 :, 3 * ch :] = jnp.where(foot, after, tail).astype(BF16)

    def spread(r, carry):
        spread_row(1, r, 2 * r + 1)
        spread_row(0, r + 1, 2 * r + 2)
        return carry

    def mend_field(r, carry):
        mend_row(0, r, 2 * r)
        mend_row(1, r, 2 * r + 1)
        return carry

    own.wait()
    lax.fori_loop(0, half, spread, 0)
    finish_receives(halos)
    spread_row(0, 0, 0)
    spread_row(1, half, rows + 1)
    lax.fori_loop(0, half + 1, mend_field, 0)

    size = BLOCK * wide
    total = jnp.zeros((1, 2 * ch), F32)
    for e in range(2):
        for p in range(2):

            def convolve(step, carry, e=e, p=p):
                r = step * BLOCK
                acc = None
                for a in range(3):
                    lhs = taps[(e + a) % 2, pl.ds(r + (e + a) // 2, BLOCK), :, p * ch : (p + 3) * ch]
                    part = dot(lhs.reshape(size, 3 * ch), wf[a])
                    acc = part if acc is None else acc + part
                pre[e, p, pl.ds(r, BLOCK)] = acc.reshape(BLOCK, wide, 2 * ch)
                return carry + jnp.sum(acc, axis=0, keepdims=True)

            total = lax.fori_loop(0, half // BLOCK, convolve, total)
    finish_sends(halos)

    def fold(value):
        return jnp.concatenate([value[:, :ch], value[:, ch:]], axis=0)

    cells = float(rows * cols)
    mean = total / cells

    def squares(r, carry):
        for e in range(2):
            for p in range(2):
                gap = pre[e, p, r] - mean
                carry = carry + jnp.sum(gap * gap, axis=0, keepdims=True)
        return carry

    spread_sum = lax.fori_loop(0, half, squares, jnp.zeros((1, 2 * ch), F32))

    def everyone(source, target, ssem, rsem):
        def start(k, carry):
            to = lax.rem(me + k, devices)
            remote(source(to), target.at[me], ssem.at[k], rsem.at[k], place(to)).start()
            return carry

        def receive(k, carry):
            at = lax.rem(me + devices - k, devices)
            remote(source(at), target.at[at], ssem.at[k], rsem.at[k], place(at)).wait_recv()
            return carry

        def sent(k, carry):
            to = lax.rem(me + k, devices)
            remote(source(to), target.at[me], ssem.at[k], rsem.at[k], place(to)).wait_send()
            return carry

        return (
            lambda: lax.fori_loop(1, devices, start, 0),
            lambda: lax.fori_loop(1, devices, receive, 0),
            lambda: lax.fori_loop(1, devices, sent, 0),
        )

    def grouped(value):
        return jnp.dot(value, member, precision=HIGH, preferred_element_type=F32)

    per_group = ch // GROUPS
    count = cells * devices * per_group
    stat_a[me] = jnp.concatenate([fold(mean), fold(spread_sum), jnp.zeros((4, ch), F32)], axis=0)
    go, receive, sent_a = everyone(lambda to: stat_a.at[me], stat_a, sa_s, sa_r)
    go()
    receive()
    stats = stat_a[...]
    centre8 = grouped(jnp.sum(stats, axis=0)) / float(devices * per_group)
    centre2 = centre8[0:2]
    drift = stats[:, 0:2] - centre2[None]
    moment = jnp.sum(stats[:, 2:4] + cells * (drift * drift), axis=0)
    variance = grouped(jnp.concatenate([moment, jnp.zeros((6, ch), F32)], axis=0))[0:2] / count
    inv2 = lax.rsqrt(variance + EPS)
    centre_s, inv_s = centre2[1:2], inv2[1:2]
    centre_both = jnp.concatenate([centre2[0:1], centre_s], axis=1)
    inv_both = jnp.concatenate([inv2[0:1], inv_s], axis=1)
    gain_both = jnp.concatenate([gain, gain], axis=1)
    bias_both = jnp.concatenate([bias, bias], axis=1)

    crest = lax.broadcasted_iota(jnp.int32, (wide, 2 * ch), 0) == 0

    def activate(r, carry):
        for e in range(2):
            at = r + 1 if e else r + half + 1
            for p in range(2):
                normed = (pre[e, p, r] - centre_both) * inv_both * gain_both + bias_both
                value = normed * jax.nn.sigmoid(normed)
                rounded = value.astype(BF16)
                for net in range(2):
                    hid[net, at, :, (p + 1) * ch : (p + 2) * ch] = rounded[:, net * ch : (net + 1) * ch]
                if p:
                    value = rounded.astype(F32)
                    hcol[pl.ds(e * half + r, 1), :] = value[wide - 1 :, :]
                    rolled = jnp.where(crest, 0.0, pltpu.roll(value, 1, 0)).astype(BF16)
                    for net in range(2):
                        hid[net, at, :, :ch] = rolled[:, net * ch : (net + 1) * ch]
        return carry

    lax.fori_loop(0, half, activate, 0)
    hids = [
        (remote(hid.at[:, half], hrow_in, hid_s.at[0], hid_r.at[0], (down, lon)), has_down, has_up),
        (remote(hcol, hcol_in, hid_s.at[1], hid_r.at[1], (lat, east)), None, None),
        (remote(hcol.at[pl.ds(rows - 8, 8)], hcorner, hid_s.at[2], hid_r.at[2], (down, east)), has_down, has_up),
    ]
    begin(hids)
    sent_a()

    @pl.when(jnp.logical_not(has_up))
    def _():
        hrow_in[...] = jnp.zeros(hrow_in.shape, BF16)
        hcorner[...] = jnp.zeros(hcorner.shape, F32)

    hid[:, 0] = jnp.zeros((2, wide, 3 * ch), BF16)
    starts = (0, half + 1, 1)
    scale = LOSS_WEIGHT / float(half * wide * devices)

    def shrink(step, carry):
        r = step * BLOCK
        for net in range(2):
            acc = None
            for a in range(3):
                lhs = hid[net, pl.ds(r + starts[a], BLOCK)].reshape(size, 3 * ch)
                part = dot(lhs, wd[net, a])
                acc = part if acc is None else acc + part
            outs[net, pl.ds(r, BLOCK)] = acc.reshape(BLOCK, wide, out_ch)
        return carry

    lax.fori_loop(0, half // BLOCK, shrink, 0)
    finish_sends(hids)
    finish_receives(hids)
    west_even, west_odd = hcol_in[:half, :], hcol_in[half:, :]
    west_last = jnp.concatenate([hcorner[7:8, :], west_odd[: half - 1]], axis=0)
    for net in range(2):
        here = slice(net * ch, (net + 1) * ch)
        acc = dot(hrow_in[net], wd[net, 0])
        outs[net, 0] = outs[net, 0] + acc
        acc = None
        for a, value in enumerate((west_last, west_even, west_odd)):
            part = dot(value[:, here].astype(BF16), wd[net, a, :ch])
            acc = part if acc is None else acc + part
        edge[net] = acc
    start_col = lax.broadcasted_iota(jnp.int32, (wide, out_ch), 0) == 0

    def finish_row(r, carry):
        both = []
        for net in range(2):
            extra = jnp.broadcast_to(edge[net, pl.ds(r, 1), :], (wide, out_ch))
            both.append(outs[net, r] + jnp.where(start_col, extra, 0.0))
        out_ref[r] = both[1].astype(BF16)
        ct = (scale * (both[1] - both[0])).astype(BF16)
        cot[r, :, :out_ch] = ct
        line = ct.astype(F32)
        ccol[pl.ds(r, 1), :] = line[0:1]
        cot[r, :, out_ch:] = pltpu.roll(line, wide - 1, 0).astype(BF16)
        return carry

    lax.fori_loop(0, half, finish_row, 0)
    cots = [
        (remote(cot.at[0], cot.at[half], cot_s.at[0], cot_r.at[0], (up, lon)), has_up, has_down),
        (remote(ccol, ccol_in, cot_s.at[1], cot_r.at[1], (lat, west)), None, None),
        (remote(ccol.at[pl.ds(0, 8)], ccorner, cot_s.at[2], cot_r.at[2], (up, west)), has_up, has_down),
    ]
    begin(cots)

    @pl.when(jnp.logical_not(has_down))
    def _():
        cot[half] = jnp.zeros((wide, 2 * out_ch), BF16)
        ccorner[...] = jnp.zeros(ccorner.shape, F32)

    for step in range(half // BLOCK):
        piece = cot[step * BLOCK : (step + 1) * BLOCK, :, :out_ch].reshape(size, out_ch)
        cturn[:, step * size : (step + 1) * size] = piece.astype(F32).T.astype(BF16)
    def put_west(at, value):
        tile = hid[1, at, :16, :ch].astype(F32)
        new = jnp.broadcast_to(value[:, ch:], (16, ch))
        hid[1, at, :16, :ch] = jnp.where(top, new, tile).astype(BF16)

    def mend(r, carry):
        put_west(r + half + 1, hcol_in[pl.ds(r, 1), :])
        put_west(r + 1, hcol_in[pl.ds(r + half, 1), :])
        return carry

    hid[1, 0] = hrow_in[1]
    lax.fori_loop(0, half, mend, 0)
    put_west(0, hcorner[7:8, :])
    gd[9 * ch :, :] = jnp.zeros((16, out_ch), F32)
    gf[9 * ch :, :] = jnp.zeros((16, ch), F32)
    for a in range(3):
        turned = dot(cturn[...], hid[1, starts[a] : starts[a] + half].reshape(half * wide, 3 * ch))
        for b in range(3):
            at = (a * 3 + b) * ch
            gd[at : at + ch, :] = turned[:, b * ch : (b + 1) * ch].T * mask_down
    finish_sends(cots)
    finish_receives(cots)
    bottom = lax.broadcasted_iota(jnp.int32, (16, out_ch), 0) == 15

    def put_east(at, value):
        tile = cot[at, wide - 16 :, out_ch:].astype(F32)
        cot[at, wide - 16 :, out_ch:] = jnp.where(bottom, jnp.broadcast_to(value, (16, out_ch)), tile).astype(BF16)

    def mend_east(r, carry):
        put_east(r, ccol_in[pl.ds(r, 1), :])
        return carry

    lax.fori_loop(0, half, mend_east, 0)
    put_east(half, ccorner[0:1, :])

    def backward(step, carry):
        r = step * BLOCK
        here = cot[pl.ds(r, BLOCK)].reshape(size, 2 * out_ch)
        after = cot[pl.ds(r + 1, BLOCK)].reshape(size, 2 * out_ch)
        pair = (dot(here, wt[1]), dot(here, wt[2]) + dot(after, wt[0]))
        one, two = carry
        for e in range(2):
            for p in range(2):
                hat = (pre[e, p, pl.ds(r, BLOCK), :, ch:].reshape(size, ch) - centre_s) * inv_s
                normed = hat * gain + bias
                sigma = jax.nn.sigmoid(normed)
                value = pair[e][:, p * ch : (p + 1) * ch] * sigma * (1.0 + normed * (1.0 - sigma)) * gain
                ghat[e, pl.ds(r, BLOCK), :, p * ch : (p + 1) * ch] = value.reshape(BLOCK, wide, ch)
                one = one + jnp.sum(value, axis=0, keepdims=True)
                two = two + jnp.sum(value * hat, axis=0, keepdims=True)
        return one, two

    zero = jnp.zeros((1, ch), F32)
    one, two = lax.fori_loop(0, half // BLOCK, backward, (zero, zero))
    stat_b[me] = jnp.concatenate([one, two, jnp.zeros((6, ch), F32)], axis=0)
    go, receive_b, sent_b = everyone(lambda to: stat_b.at[me], stat_b, sb_s, sb_r)
    go()

    pairs = devices // 2
    core = lax.rem(lon, 2)
    mine = me // 2
    mate = (lat, lon + 1 - 2 * core)

    def pack(grads, buffer):
        for d in range(devices):
            buffer[d % 2, d // 2] = grads[d * chunk : d * chunk + padded, :].astype(BF16)

    def merge(buffer, other, merged, got):
        def one_chunk(h, carry):
            merged[h] = (buffer[core, h].astype(F32) + other[h].astype(F32)).astype(BF16)
            return carry

        lax.fori_loop(0, pairs, one_chunk, 0)
        got[mine] = merged[mine]

    def scatter(merged, got, ssem, rsem):
        def owner(h):
            return place(2 * h + core)

        def start(k, carry):
            to = lax.rem(mine + k, pairs)
            remote(merged.at[to], got.at[mine], ssem.at[k], rsem.at[k], owner(to)).start()
            return carry

        def receive(k, carry):
            at = lax.rem(mine + pairs - k, pairs)
            remote(merged.at[at], got.at[at], ssem.at[k], rsem.at[k], owner(at)).wait_recv()
            return carry

        def sent(k, carry):
            to = lax.rem(mine + k, pairs)
            remote(merged.at[to], got.at[mine], ssem.at[k], rsem.at[k], owner(to)).wait_send()
            return carry

        return (
            lambda: lax.fori_loop(1, pairs, start, 0),
            lambda: lax.fori_loop(1, pairs, receive, 0),
            lambda: lax.fori_loop(1, pairs, sent, 0),
        )

    pack(gd, send_d)
    swap_d = remote(send_d.at[1 - core], other_d, swap_s.at[0], swap_r.at[0], mate)
    swap_d.start()
    go_d, receive_d, sent_d = scatter(merged_d, got_d, rd_s, rd_r)

    receive_b()
    back = grouped(jnp.sum(stat_b[...], axis=0)) / count
    m1, m2 = back[0:1], back[1:2]
    for e in range(2):
        for step in range(half // BLOCK):
            r = step * BLOCK
            for p in range(2):
                hat = (pre[e, p, r : r + BLOCK, :, ch:].reshape(size, ch) - centre_s) * inv_s
                value = ghat[e, r : r + BLOCK, :, p * ch : (p + 1) * ch].reshape(size, ch)
                gpre = inv_s * (value - m1 - hat * m2)
                gturn[e, p * ch : (p + 1) * ch, step * size : (step + 1) * size] = gpre.T.astype(BF16)
    swap_d.wait_recv()
    merge(send_d, other_d, merged_d, got_d)
    go_d()
    for a in range(3):
        acc = None
        for e in range(2):
            start = (e + a) // 2
            part = dot(gturn[e], taps[(e + a) % 2, start : start + half].reshape(half * wide, 4 * ch))
            acc = part if acc is None else acc + part
        for b in range(3):
            at = (a * 3 + b) * ch
            block = acc[:ch, b * ch : (b + 1) * ch] + acc[ch:, (b + 1) * ch : (b + 2) * ch]
            gf[at : at + ch, :] = block.T * mask_first
    pack(gf, send_f)
    swap_f = remote(send_f.at[1 - core], other_f, swap_s.at[1], swap_r.at[1], mate)
    swap_f.start()
    go_f, receive_f, sent_f = scatter(merged_f, got_f, rf_s, rf_r)

    def add_up(got, width):
        def add(d, acc):
            return acc + got[d].astype(F32)

        return lax.fori_loop(0, pairs, add, jnp.zeros((padded, width), F32))[:chunk]

    swap_f.wait_recv()
    merge(send_f, other_f, merged_f, got_f)
    go_f()
    receive_d()
    gdown_ref[...] = add_up(got_d, out_ch)
    receive_f()
    gfirst_ref[...] = add_up(got_f, ch)
    sent_b()
    sent_d()
    sent_f()
    swap_d.wait_send()
    swap_f.wait_send()


def local(nlat, nlon, field, w_first, w_down, keep_first, chan_first, keep_down, chan_down, group_ids, norm_gain, norm_bias):
    rows, cols, ch = field.shape
    out_ch = w_down.shape[3]
    devices = nlat * nlon
    pairs = devices // 2
    half, wide = rows // 2, cols // 2
    chunk = 9 * ch // devices
    padded = -(-chunk // 16) * 16
    vmem = pl.BlockSpec(memory_space=pltpu.VMEM)
    dma = pltpu.SemaphoreType.DMA
    S = pltpu.VMEM
    return tuple(
        pl.pallas_call(
            functools.partial(kernel, nlat, nlon, chunk, padded),
            out_shape=(
                jax.ShapeDtypeStruct((half, wide, out_ch), BF16),
                jax.ShapeDtypeStruct((chunk, ch), F32),
                jax.ShapeDtypeStruct((chunk, out_ch), F32),
            ),
            in_specs=[pl.BlockSpec(memory_space=pl.ANY)] + [vmem] * 9,
            out_specs=(vmem, vmem, vmem),
            scratch_shapes=[
                S((rows + 2, cols + 32, ch), BF16),
                S((2, cols + 32, ch), F32),
                S((2, half + 1, wide, 4 * ch), BF16),
                S((2, 2, half, wide, 2 * ch), F32),
                S((2, rows + 1, wide, 3 * ch), BF16),
                S((rows, 2 * ch), F32),
                S((rows, 2 * ch), F32),
                S((8, 2 * ch), F32),
                S((2, wide, 3 * ch), BF16),
                S((2, half, wide, out_ch), F32),
                S((2, half, out_ch), F32),
                S((half + 1, wide, 2 * out_ch), BF16),
                S((half, out_ch), F32),
                S((half, out_ch), F32),
                S((8, out_ch), F32),
                S((2, half, wide, 2 * ch), F32),
                S((2, 2 * ch, half * wide), BF16),
                S((out_ch, half * wide), BF16),
                S((3, 3 * ch, 2 * ch), BF16),
                S((2, 3, 3 * ch, out_ch), BF16),
                S((3, 2 * out_ch, 2 * ch), BF16),
                S((9 * ch + 16, ch), F32),
                S((9 * ch + 16, out_ch), F32),
                S((2, pairs, padded, ch), BF16),
                S((2, pairs, padded, out_ch), BF16),
                S((pairs, padded, ch), BF16),
                S((pairs, padded, out_ch), BF16),
                S((pairs, padded, ch), BF16),
                S((pairs, padded, out_ch), BF16),
                S((pairs, padded, ch), BF16),
                S((pairs, padded, out_ch), BF16),
                S((devices, 8, ch), F32),
                S((devices, 8, ch), F32),
                dma,
                dma((8,)), dma((8,)),
                dma((3,)), dma((3,)),
                dma((3,)), dma((3,)),
                dma((devices,)), dma((devices,)),
                dma((devices,)), dma((devices,)),
                dma((2,)), dma((2,)),
                dma((pairs,)), dma((pairs,)),
                dma((pairs,)), dma((pairs,)),
            ],
            compiler_params=pltpu.CompilerParams(
                collective_id=0, has_side_effects=True, vmem_limit_bytes=56 * 1024 * 1024
            ),
        )(
            field,
            w_first,
            w_down,
            keep_first,
            chan_first.reshape(1, ch),
            keep_down,
            chan_down.reshape(1, out_ch),
            group_ids.reshape(1, ch),
            norm_gain.reshape(1, ch),
            norm_bias.reshape(1, ch),
        )
    )


def solution(mesh):
    return jax.shard_map(
        functools.partial(local, mesh.shape["lat"], mesh.shape["lon"]),
        mesh=mesh,
        in_specs=(P("lat", "lon", None), P(), P(), P(), P(), P(), P(), P(), P(), P()),
        out_specs=(P("lat", "lon", None), P(("lat", "lon"), None), P(("lat", "lon"), None)),
        check_vma=False,
    )
```

```python
import functools

import jax
import jax.numpy as jnp
from jax import lax
from jax.experimental import pallas as pl
from jax.experimental.pallas import tpu as pltpu
from jax.sharding import PartitionSpec as P

GROUPS = 32
EPS = 1e-05
LOSS_WEIGHT = 64.0
MESH = pl.DeviceIdType.MESH
F32 = jnp.float32
BF16 = jnp.bfloat16
HIGH = lax.Precision.HIGHEST
BLOCK = 16


def dot(a, b):
    return jnp.dot(a, b, preferred_element_type=F32)


def kernel(
    nlat, nlon, chunk, padded,
    field, w_first, w_down, keep_first, chan_first, keep_down, chan_down, group_ids, gain_ref, bias_ref,
    out_ref, gfirst_ref, gdown_ref,
    ext, tmp, taps, pre, hid, hcol, hcol_in, hcorner, hrow_in, outs, edge, cot, ccol, ccol_in, ccorner, ghat, gturn, cturn,
    wf, wd, wt, gf, gd, send_f, send_d, other_f, other_d, merged_f, merged_d, got_f, got_d, stat_a, stat_b,
    own_sem, halo_s, halo_r, hid_s, hid_r, cot_s, cot_r, sa_s, sa_r, sb_s, sb_r, swap_s, swap_r, rf_s, rf_r, rd_s, rd_r,
):
    devices = nlat * nlon
    rows, cols, ch = field.shape
    out_ch = w_down.shape[3]
    half, wide = rows // 2, cols // 2
    lat, lon = lax.axis_index("lat"), lax.axis_index("lon")
    me = lat * nlon + lon
    west, east = lax.rem(lon + nlon - 1, nlon), lax.rem(lon + 1, nlon)
    has_up, has_down = lat > 0, lat < nlat - 1

    def place(index):
        return (index // nlon, lax.rem(index, nlon))

    own = pltpu.make_async_copy(field, ext.at[pl.ds(1, rows), pl.ds(16, cols)], own_sem)
    own.start()

    barrier = pltpu.get_barrier_semaphore()

    def greet(k, carry):
        pl.semaphore_signal(barrier, inc=1, device_id=place(lax.rem(me + k, devices)), device_id_type=MESH)
        return carry

    lax.fori_loop(1, devices, greet, 0)
    pl.semaphore_wait(barrier, devices - 1)

    def remote(src, dst, ssem, rsem, target):
        return pltpu.make_async_remote_copy(
            src_ref=src, dst_ref=dst, send_sem=ssem, recv_sem=rsem, device_id=target, device_id_type=MESH
        )

    def guarded(condition, action):
        if condition is None:
            action()
        else:
            pl.when(condition)(action)

    def begin(plans):
        for copy, sends, _ in plans:
            guarded(sends, copy.start)

    def finish_sends(plans):
        for copy, sends, _ in plans:
            guarded(sends, copy.wait_send)

    def finish_receives(plans):
        for copy, _, receives in plans:
            guarded(receives, copy.wait_recv)

    up, down = jnp.maximum(lat - 1, 0), jnp.minimum(lat + 1, nlat - 1)
    left, right, centre = pl.ds(0, 16), pl.ds(cols - 16, 16), pl.ds(16, cols)
    far = pl.ds(16 + cols, 16)
    first, last = pl.ds(0, 1), pl.ds(rows - 1, 1)
    below = pl.ds(rows + 1, 1)

    def halo(i, src, dst, target, sends, receives):
        return (remote(src, dst, halo_s.at[i], halo_r.at[i], target), sends, receives)

    halos = [
        halo(0, field.at[first], ext.at[below, centre], (up, lon), has_up, has_down),
        halo(1, field.at[last], ext.at[first, centre], (down, lon), has_down, has_up),
        halo(2, field.at[:, left], ext.at[pl.ds(1, rows), far], (lat, west), None, None),
        halo(3, field.at[:, right], ext.at[pl.ds(1, rows), left], (lat, east), None, None),
        halo(4, field.at[first, left], ext.at[below, far], (up, west), has_up, has_down),
        halo(5, field.at[first, right], ext.at[below, left], (up, east), has_up, has_down),
        halo(6, field.at[last, left], ext.at[first, far], (down, west), has_down, has_up),
        halo(7, field.at[last, right], ext.at[first, left], (down, east), has_down, has_up),
    ]
    begin(halos)

    @pl.when(jnp.logical_not(has_up))
    def _():
        ext[0] = jnp.zeros(ext.shape[1:], BF16)

    @pl.when(jnp.logical_not(has_down))
    def _():
        ext[rows + 1] = jnp.zeros(ext.shape[1:], BF16)

    mask_first = (keep_first[...] * chan_first[...]).astype(F32)
    mask_down = (keep_down[...] * chan_down[...]).astype(F32)
    for a in range(3):
        wt[a, out_ch:, :ch] = jnp.zeros((out_ch, ch), BF16)
        for b in range(3):
            here = slice(b * ch, (b + 1) * ch)
            wf[a, here, :ch] = w_first[a, b]
            wf[a, here, ch:] = (w_first[a, b].astype(F32) * mask_first).astype(BF16)
            student = w_down[a, b].astype(F32) * mask_down
            wd[0, a, here] = w_down[a, b]
            wd[1, a, here] = student.astype(BF16)
            turned = student.T.astype(BF16)
            if b == 0:
                wt[a, out_ch:, ch:] = turned
            elif b == 1:
                wt[a, :out_ch, :ch] = turned
            else:
                wt[a, :out_ch, ch:] = turned
    ids = jnp.broadcast_to(group_ids[...].astype(F32), (ch, ch))
    member = (ids == ids.T).astype(F32)
    gain, bias = gain_ref[...], bias_ref[...]

    top = lax.broadcasted_iota(jnp.int32, (16, ch), 0) == 0
    foot = lax.broadcasted_iota(jnp.int32, (16, ch), 0) == 15
    tmp[...] = jnp.zeros(tmp.shape, F32)

    def spread_row(e, r, at):
        tmp[e, 16 : 16 + cols] = ext[at, 16 : 16 + cols].astype(F32)
        for k in range(4):
            taps[e, r, :, k * ch : (k + 1) * ch] = tmp[e, pl.ds(15 + k, wide, stride=2), :].astype(BF16)

    def mend_row(e, r, at):
        before = pltpu.roll(ext[at, :16].astype(F32), 1, 0)
        after = pltpu.roll(ext[at, 16 + cols :].astype(F32), 15, 0)
        head = taps[e, r, :16, :ch].astype(F32)
        tail = taps[e, r, wide - 16 :, 3 * ch :].astype(F32)
        taps[e, r, :16, :ch] = jnp.where(top, before, head).astype(BF16)
        taps[e, r, wide - 16 :, 3 * ch :] = jnp.where(foot, after, tail).astype(BF16)

    def spread(r, carry):
        spread_row(1, r, 2 * r + 1)
        spread_row(0, r + 1, 2 * r + 2)
        return carry

    def mend_field(r, carry):
        mend_row(0, r, 2 * r)
        mend_row(1, r, 2 * r + 1)
        return carry

    own.wait()
    lax.fori_loop(0, half, spread, 0)
    finish_receives(halos)
    spread_row(0, 0, 0)
    spread_row(1, half, rows + 1)
    lax.fori_loop(0, half + 1, mend_field, 0)

    size = BLOCK * wide
    total = jnp.zeros((1, 2 * ch), F32)
    for e in range(2):
        for p in range(2):

            def convolve(step, carry, e=e, p=p):
                r = step * BLOCK
                acc = None
                for a in range(3):
                    lhs = taps[(e + a) % 2, pl.ds(r + (e + a) // 2, BLOCK), :, p * ch : (p + 3) * ch]
                    part = dot(lhs.reshape(size, 3 * ch), wf[a])
                    acc = part if acc is None else acc + part
                pre[e, p, pl.ds(r, BLOCK)] = acc.reshape(BLOCK, wide, 2 * ch)
                return carry + jnp.sum(acc, axis=0, keepdims=True)

            total = lax.fori_loop(0, half // BLOCK, convolve, total)
    finish_sends(halos)

    def fold(value):
        return jnp.concatenate([value[:, :ch], value[:, ch:]], axis=0)

    cells = float(rows * cols)
    mean = total / cells

    def squares(r, carry):
        for e in range(2):
            for p in range(2):
                gap = pre[e, p, r] - mean
                carry = carry + jnp.sum(gap * gap, axis=0, keepdims=True)
        return carry

    spread_sum = lax.fori_loop(0, half, squares, jnp.zeros((1, 2 * ch), F32))

    def everyone(source, target, ssem, rsem):
        def start(k, carry):
            to = lax.rem(me + k, devices)
            remote(source(to), target.at[me], ssem.at[k], rsem.at[k], place(to)).start()
            return carry

        def receive(k, carry):
            at = lax.rem(me + devices - k, devices)
            remote(source(at), target.at[at], ssem.at[k], rsem.at[k], place(at)).wait_recv()
            return carry

        def sent(k, carry):
            to = lax.rem(me + k, devices)
            remote(source(to), target.at[me], ssem.at[k], rsem.at[k], place(to)).wait_send()
            return carry

        return (
            lambda: lax.fori_loop(1, devices, start, 0),
            lambda: lax.fori_loop(1, devices, receive, 0),
            lambda: lax.fori_loop(1, devices, sent, 0),
        )

    def grouped(value):
        return jnp.dot(value, member, precision=HIGH, preferred_element_type=F32)

    per_group = ch // GROUPS
    count = cells * devices * per_group
    stat_a[me] = jnp.concatenate([fold(mean), fold(spread_sum), jnp.zeros((4, ch), F32)], axis=0)
    go, receive, sent_a = everyone(lambda to: stat_a.at[me], stat_a, sa_s, sa_r)
    go()
    receive()
    stats = stat_a[...]
    centre8 = grouped(jnp.sum(stats, axis=0)) / float(devices * per_group)
    centre2 = centre8[0:2]
    drift = stats[:, 0:2] - centre2[None]
    moment = jnp.sum(stats[:, 2:4] + cells * (drift * drift), axis=0)
    variance = grouped(jnp.concatenate([moment, jnp.zeros((6, ch), F32)], axis=0))[0:2] / count
    inv2 = lax.rsqrt(variance + EPS)
    centre_s, inv_s = centre2[1:2], inv2[1:2]
    centre_both = jnp.concatenate([centre2[0:1], centre_s], axis=1)
    inv_both = jnp.concatenate([inv2[0:1], inv_s], axis=1)
    gain_both = jnp.concatenate([gain, gain], axis=1)
    bias_both = jnp.concatenate([bias, bias], axis=1)

    crest = lax.broadcasted_iota(jnp.int32, (wide, 2 * ch), 0) == 0

    def activate(r, carry):
        for e in range(2):
            at = r + 1 if e else r + half + 1
            for p in range(2):
                normed = (pre[e, p, r] - centre_both) * inv_both * gain_both + bias_both
                value = normed * jax.nn.sigmoid(normed)
                rounded = value.astype(BF16)
                for net in range(2):
                    hid[net, at, :, (p + 1) * ch : (p + 2) * ch] = rounded[:, net * ch : (net + 1) * ch]
                if p:
                    value = rounded.astype(F32)
                    hcol[pl.ds(e * half + r, 1), :] = value[wide - 1 :, :]
                    rolled = jnp.where(crest, 0.0, pltpu.roll(value, 1, 0)).astype(BF16)
                    for net in range(2):
                        hid[net, at, :, :ch] = rolled[:, net * ch : (net + 1) * ch]
        return carry

    lax.fori_loop(0, half, activate, 0)
    hids = [
        (remote(hid.at[:, half], hrow_in, hid_s.at[0], hid_r.at[0], (down, lon)), has_down, has_up),
        (remote(hcol, hcol_in, hid_s.at[1], hid_r.at[1], (lat, east)), None, None),
        (remote(hcol.at[pl.ds(rows - 8, 8)], hcorner, hid_s.at[2], hid_r.at[2], (down, east)), has_down, has_up),
    ]
    begin(hids)
    sent_a()

    @pl.when(jnp.logical_not(has_up))
    def _():
        hrow_in[...] = jnp.zeros(hrow_in.shape, BF16)
        hcorner[...] = jnp.zeros(hcorner.shape, F32)

    hid[:, 0] = jnp.zeros((2, wide, 3 * ch), BF16)
    starts = (0, half + 1, 1)
    scale = LOSS_WEIGHT / float(half * wide * devices)

    def shrink(step, carry):
        r = step * BLOCK
        for net in range(2):
            acc = None
            for a in range(3):
                lhs = hid[net, pl.ds(r + starts[a], BLOCK)].reshape(size, 3 * ch)
                part = dot(lhs, wd[net, a])
                acc = part if acc is None else acc + part
            outs[net, pl.ds(r, BLOCK)] = acc.reshape(BLOCK, wide, out_ch)
        return carry

    lax.fori_loop(0, half // BLOCK, shrink, 0)
    finish_sends(hids)
    finish_receives(hids)
    west_even, west_odd = hcol_in[:half, :], hcol_in[half:, :]
    west_last = jnp.concatenate([hcorner[7:8, :], west_odd[: half - 1]], axis=0)
    for net in range(2):
        here = slice(net * ch, (net + 1) * ch)
        acc = dot(hrow_in[net], wd[net, 0])
        outs[net, 0] = outs[net, 0] + acc
        acc = None
        for a, value in enumerate((west_last, west_even, west_odd)):
            part = dot(value[:, here].astype(BF16), wd[net, a, :ch])
            acc = part if acc is None else acc + part
        edge[net] = acc
    start_col = lax.broadcasted_iota(jnp.int32, (wide, out_ch), 0) == 0

    def finish_row(r, carry):
        both = []
        for net in range(2):
            extra = jnp.broadcast_to(edge[net, pl.ds(r, 1), :], (wide, out_ch))
            both.append(outs[net, r] + jnp.where(start_col, extra, 0.0))
        out_ref[r] = both[1].astype(BF16)
        ct = (scale * (both[1] - both[0])).astype(BF16)
        cot[r, :, :out_ch] = ct
        line = ct.astype(F32)
        ccol[pl.ds(r, 1), :] = line[0:1]
        cot[r, :, out_ch:] = pltpu.roll(line, wide - 1, 0).astype(BF16)
        return carry

    lax.fori_loop(0, half, finish_row, 0)
    cots = [
        (remote(cot.at[0], cot.at[half], cot_s.at[0], cot_r.at[0], (up, lon)), has_up, has_down),
        (remote(ccol, ccol_in, cot_s.at[1], cot_r.at[1], (lat, west)), None, None),
        (remote(ccol.at[pl.ds(0, 8)], ccorner, cot_s.at[2], cot_r.at[2], (up, west)), has_up, has_down),
    ]
    begin(cots)

    @pl.when(jnp.logical_not(has_down))
    def _():
        cot[half] = jnp.zeros((wide, 2 * out_ch), BF16)
        ccorner[...] = jnp.zeros(ccorner.shape, F32)

    for step in range(half // BLOCK):
        piece = cot[step * BLOCK : (step + 1) * BLOCK, :, :out_ch].reshape(size, out_ch)
        cturn[:, step * size : (step + 1) * size] = piece.astype(F32).T.astype(BF16)
    def put_west(at, value):
        tile = hid[1, at, :16, :ch].astype(F32)
        new = jnp.broadcast_to(value[:, ch:], (16, ch))
        hid[1, at, :16, :ch] = jnp.where(top, new, tile).astype(BF16)

    def mend(r, carry):
        put_west(r + half + 1, hcol_in[pl.ds(r, 1), :])
        put_west(r + 1, hcol_in[pl.ds(r + half, 1), :])
        return carry

    hid[1, 0] = hrow_in[1]
    lax.fori_loop(0, half, mend, 0)
    put_west(0, hcorner[7:8, :])
    gd[9 * ch :, :] = jnp.zeros((16, out_ch), F32)
    gf[9 * ch :, :] = jnp.zeros((16, ch), F32)
    for a in range(3):
        turned = dot(cturn[...], hid[1, starts[a] : starts[a] + half].reshape(half * wide, 3 * ch))
        for b in range(3):
            at = (a * 3 + b) * ch
            gd[at : at + ch, :] = turned[:, b * ch : (b + 1) * ch].T * mask_down
    pairs = devices // 2
    core = lax.rem(lon, 2)
    mine = me // 2
    mate = (lat, lon + 1 - 2 * core)

    def pack(grads, buffer):
        for d in range(devices):
            buffer[d % 2, d // 2] = grads[d * chunk : d * chunk + padded, :].astype(BF16)

    def merge(buffer, other, merged, got):
        def one_chunk(h, carry):
            merged[h] = (buffer[core, h].astype(F32) + other[h].astype(F32)).astype(BF16)
            return carry

        lax.fori_loop(0, pairs, one_chunk, 0)
        got[mine] = merged[mine]

    def scatter(merged, got, ssem, rsem):
        def owner(h):
            return place(2 * h + core)

        def start(k, carry):
            to = lax.rem(mine + k, pairs)
            remote(merged.at[to], got.at[mine], ssem.at[k], rsem.at[k], owner(to)).start()
            return carry

        def receive(k, carry):
            at = lax.rem(mine + pairs - k, pairs)
            remote(merged.at[at], got.at[at], ssem.at[k], rsem.at[k], owner(at)).wait_recv()
            return carry

        def sent(k, carry):
            to = lax.rem(mine + k, pairs)
            remote(merged.at[to], got.at[mine], ssem.at[k], rsem.at[k], owner(to)).wait_send()
            return carry

        return (
            lambda: lax.fori_loop(1, pairs, start, 0),
            lambda: lax.fori_loop(1, pairs, receive, 0),
            lambda: lax.fori_loop(1, pairs, sent, 0),
        )

    pack(gd, send_d)
    swap_d = remote(send_d.at[1 - core], other_d, swap_s.at[0], swap_r.at[0], mate)
    swap_d.start()
    finish_sends(cots)
    finish_receives(cots)
    bottom = lax.broadcasted_iota(jnp.int32, (16, out_ch), 0) == 15

    def put_east(at, value):
        tile = cot[at, wide - 16 :, out_ch:].astype(F32)
        cot[at, wide - 16 :, out_ch:] = jnp.where(bottom, jnp.broadcast_to(value, (16, out_ch)), tile).astype(BF16)

    def mend_east(r, carry):
        put_east(r, ccol_in[pl.ds(r, 1), :])
        return carry

    lax.fori_loop(0, half, mend_east, 0)
    put_east(half, ccorner[0:1, :])

    def backward(step, carry):
        r = step * BLOCK
        here = cot[pl.ds(r, BLOCK)].reshape(size, 2 * out_ch)
        after = cot[pl.ds(r + 1, BLOCK)].reshape(size, 2 * out_ch)
        pair = (dot(here, wt[1]), dot(here, wt[2]) + dot(after, wt[0]))
        one, two = carry
        for e in range(2):
            for p in range(2):
                hat = (pre[e, p, pl.ds(r, BLOCK), :, ch:].reshape(size, ch) - centre_s) * inv_s
                normed = hat * gain + bias
                sigma = jax.nn.sigmoid(normed)
                value = pair[e][:, p * ch : (p + 1) * ch] * sigma * (1.0 + normed * (1.0 - sigma)) * gain
                ghat[e, pl.ds(r, BLOCK), :, p * ch : (p + 1) * ch] = value.reshape(BLOCK, wide, ch)
                one = one + jnp.sum(value, axis=0, keepdims=True)
                two = two + jnp.sum(value * hat, axis=0, keepdims=True)
        return one, two

    zero = jnp.zeros((1, ch), F32)
    one, two = lax.fori_loop(0, half // BLOCK, backward, (zero, zero))
    stat_b[me] = jnp.concatenate([one, two, jnp.zeros((6, ch), F32)], axis=0)
    go, receive_b, sent_b = everyone(lambda to: stat_b.at[me], stat_b, sb_s, sb_r)
    go()

    go_d, receive_d, sent_d = scatter(merged_d, got_d, rd_s, rd_r)

    swap_d.wait_recv()
    merge(send_d, other_d, merged_d, got_d)
    go_d()
    receive_b()
    back = grouped(jnp.sum(stat_b[...], axis=0)) / count
    m1, m2 = back[0:1], back[1:2]
    for e in range(2):
        for step in range(half // BLOCK):
            r = step * BLOCK
            for p in range(2):
                hat = (pre[e, p, r : r + BLOCK, :, ch:].reshape(size, ch) - centre_s) * inv_s
                value = ghat[e, r : r + BLOCK, :, p * ch : (p + 1) * ch].reshape(size, ch)
                gpre = inv_s * (value - m1 - hat * m2)
                gturn[e, p * ch : (p + 1) * ch, step * size : (step + 1) * size] = gpre.T.astype(BF16)
    for a in range(3):
        acc = None
        for e in range(2):
            start = (e + a) // 2
            part = dot(gturn[e], taps[(e + a) % 2, start : start + half].reshape(half * wide, 4 * ch))
            acc = part if acc is None else acc + part
        for b in range(3):
            at = (a * 3 + b) * ch
            block = acc[:ch, b * ch : (b + 1) * ch] + acc[ch:, (b + 1) * ch : (b + 2) * ch]
            gf[at : at + ch, :] = block.T * mask_first
    pack(gf, send_f)
    swap_f = remote(send_f.at[1 - core], other_f, swap_s.at[1], swap_r.at[1], mate)
    swap_f.start()
    go_f, receive_f, sent_f = scatter(merged_f, got_f, rf_s, rf_r)

    def add_up(got, width):
        def add(d, acc):
            return acc + got[d].astype(F32)

        return lax.fori_loop(0, pairs, add, jnp.zeros((padded, width), F32))[:chunk]

    swap_f.wait_recv()
    merge(send_f, other_f, merged_f, got_f)
    go_f()
    receive_d()
    gdown_ref[...] = add_up(got_d, out_ch)
    receive_f()
    gfirst_ref[...] = add_up(got_f, ch)
    sent_b()
    sent_d()
    sent_f()
    swap_d.wait_send()
    swap_f.wait_send()


def local(nlat, nlon, field, w_first, w_down, keep_first, chan_first, keep_down, chan_down, group_ids, norm_gain, norm_bias):
    rows, cols, ch = field.shape
    out_ch = w_down.shape[3]
    devices = nlat * nlon
    pairs = devices // 2
    half, wide = rows // 2, cols // 2
    chunk = 9 * ch // devices
    padded = -(-chunk // 16) * 16
    vmem = pl.BlockSpec(memory_space=pltpu.VMEM)
    dma = pltpu.SemaphoreType.DMA
    S = pltpu.VMEM
    return tuple(
        pl.pallas_call(
            functools.partial(kernel, nlat, nlon, chunk, padded),
            out_shape=(
                jax.ShapeDtypeStruct((half, wide, out_ch), BF16),
                jax.ShapeDtypeStruct((chunk, ch), F32),
                jax.ShapeDtypeStruct((chunk, out_ch), F32),
            ),
            in_specs=[pl.BlockSpec(memory_space=pl.ANY)] + [vmem] * 9,
            out_specs=(vmem, vmem, vmem),
            scratch_shapes=[
                S((rows + 2, cols + 32, ch), BF16),
                S((2, cols + 32, ch), F32),
                S((2, half + 1, wide, 4 * ch), BF16),
                S((2, 2, half, wide, 2 * ch), F32),
                S((2, rows + 1, wide, 3 * ch), BF16),
                S((rows, 2 * ch), F32),
                S((rows, 2 * ch), F32),
                S((8, 2 * ch), F32),
                S((2, wide, 3 * ch), BF16),
                S((2, half, wide, out_ch), F32),
                S((2, half, out_ch), F32),
                S((half + 1, wide, 2 * out_ch), BF16),
                S((half, out_ch), F32),
                S((half, out_ch), F32),
                S((8, out_ch), F32),
                S((2, half, wide, 2 * ch), F32),
                S((2, 2 * ch, half * wide), BF16),
                S((out_ch, half * wide), BF16),
                S((3, 3 * ch, 2 * ch), BF16),
                S((2, 3, 3 * ch, out_ch), BF16),
                S((3, 2 * out_ch, 2 * ch), BF16),
                S((9 * ch + 16, ch), F32),
                S((9 * ch + 16, out_ch), F32),
                S((2, pairs, padded, ch), BF16),
                S((2, pairs, padded, out_ch), BF16),
                S((pairs, padded, ch), BF16),
                S((pairs, padded, out_ch), BF16),
                S((pairs, padded, ch), BF16),
                S((pairs, padded, out_ch), BF16),
                S((pairs, padded, ch), BF16),
                S((pairs, padded, out_ch), BF16),
                S((devices, 8, ch), F32),
                S((devices, 8, ch), F32),
                dma,
                dma((8,)), dma((8,)),
                dma((3,)), dma((3,)),
                dma((3,)), dma((3,)),
                dma((devices,)), dma((devices,)),
                dma((devices,)), dma((devices,)),
                dma((2,)), dma((2,)),
                dma((pairs,)), dma((pairs,)),
                dma((pairs,)), dma((pairs,)),
            ],
            compiler_params=pltpu.CompilerParams(
                collective_id=0, has_side_effects=True, vmem_limit_bytes=56 * 1024 * 1024
            ),
        )(
            field,
            w_first,
            w_down,
            keep_first,
            chan_first.reshape(1, ch),
            keep_down,
            chan_down.reshape(1, out_ch),
            group_ids.reshape(1, ch),
            norm_gain.reshape(1, ch),
            norm_bias.reshape(1, ch),
        )
    )


def solution(mesh):
    return jax.shard_map(
        functools.partial(local, mesh.shape["lat"], mesh.shape["lon"]),
        mesh=mesh,
        in_specs=(P("lat", "lon", None), P(), P(), P(), P(), P(), P(), P(), P(), P()),
        out_specs=(P("lat", "lon", None), P(("lat", "lon"), None), P(("lat", "lon"), None)),
        check_vma=False,
    )
```

```python
import functools

import jax
import jax.numpy as jnp
from jax import lax
from jax.experimental import pallas as pl
from jax.experimental.pallas import tpu as pltpu
from jax.sharding import PartitionSpec as P

GROUPS = 32
EPS = 1e-05
LOSS_WEIGHT = 64.0
MESH = pl.DeviceIdType.MESH
F32 = jnp.float32
BF16 = jnp.bfloat16
HIGH = lax.Precision.HIGHEST
BLOCK = 16


def dot(a, b):
    return jnp.dot(a, b, preferred_element_type=F32)


def kernel(
    nlat, nlon, chunk, padded,
    field, w_first, w_down, keep_first, chan_first, keep_down, chan_down, group_ids, gain_ref, bias_ref,
    out_ref, gfirst_ref, gdown_ref,
    ext, tmp, taps, pre, hid, hcol, hcol_in, hcorner, hrow_in, outs, edge, cot, ccol, ccol_in, ccorner, ghat, gturn, cturn,
    wf, wd, wt, gf, gd, send_f, send_d, other_f, other_d, merged_f, merged_d, got_f, got_d, stat_a, stat_b,
    own_sem, halo_s, halo_r, hid_s, hid_r, cot_s, cot_r, sa_s, sa_r, sb_s, sb_r, swap_s, swap_r, rf_s, rf_r, rd_s, rd_r,
):
    devices = nlat * nlon
    rows, cols, ch = field.shape
    out_ch = w_down.shape[3]
    half, wide = rows // 2, cols // 2
    lat, lon = lax.axis_index("lat"), lax.axis_index("lon")
    me = lat * nlon + lon
    west, east = lax.rem(lon + nlon - 1, nlon), lax.rem(lon + 1, nlon)
    has_up, has_down = lat > 0, lat < nlat - 1

    def place(index):
        return (index // nlon, lax.rem(index, nlon))

    own = pltpu.make_async_copy(field, ext.at[pl.ds(1, rows), pl.ds(16, cols)], own_sem)
    own.start()

    barrier = pltpu.get_barrier_semaphore()

    def greet(k, carry):
        pl.semaphore_signal(barrier, inc=1, device_id=place(lax.rem(me + k, devices)), device_id_type=MESH)
        return carry

    lax.fori_loop(1, devices, greet, 0)
    pl.semaphore_wait(barrier, devices - 1)

    def remote(src, dst, ssem, rsem, target):
        return pltpu.make_async_remote_copy(
            src_ref=src, dst_ref=dst, send_sem=ssem, recv_sem=rsem, device_id=target, device_id_type=MESH
        )

    def guarded(condition, action):
        if condition is None:
            action()
        else:
            pl.when(condition)(action)

    def begin(plans):
        for copy, sends, _ in plans:
            guarded(sends, copy.start)

    def finish_sends(plans):
        for copy, sends, _ in plans:
            guarded(sends, copy.wait_send)

    def finish_receives(plans):
        for copy, _, receives in plans:
            guarded(receives, copy.wait_recv)

    up, down = jnp.maximum(lat - 1, 0), jnp.minimum(lat + 1, nlat - 1)
    left, right, centre = pl.ds(0, 16), pl.ds(cols - 16, 16), pl.ds(16, cols)
    far = pl.ds(16 + cols, 16)
    first, last = pl.ds(0, 1), pl.ds(rows - 1, 1)
    below = pl.ds(rows + 1, 1)

    def halo(i, src, dst, target, sends, receives):
        return (remote(src, dst, halo_s.at[i], halo_r.at[i], target), sends, receives)

    halos = [
        halo(0, field.at[first], ext.at[below, centre], (up, lon), has_up, has_down),
        halo(1, field.at[last], ext.at[first, centre], (down, lon), has_down, has_up),
        halo(2, field.at[:, left], ext.at[pl.ds(1, rows), far], (lat, west), None, None),
        halo(3, field.at[:, right], ext.at[pl.ds(1, rows), left], (lat, east), None, None),
        halo(4, field.at[first, left], ext.at[below, far], (up, west), has_up, has_down),
        halo(5, field.at[first, right], ext.at[below, left], (up, east), has_up, has_down),
        halo(6, field.at[last, left], ext.at[first, far], (down, west), has_down, has_up),
        halo(7, field.at[last, right], ext.at[first, left], (down, east), has_down, has_up),
    ]
    begin(halos)

    @pl.when(jnp.logical_not(has_up))
    def _():
        ext[0] = jnp.zeros(ext.shape[1:], BF16)

    @pl.when(jnp.logical_not(has_down))
    def _():
        ext[rows + 1] = jnp.zeros(ext.shape[1:], BF16)

    mask_first = (keep_first[...] * chan_first[...]).astype(F32)
    mask_down = (keep_down[...] * chan_down[...]).astype(F32)
    for a in range(3):
        wt[a, out_ch:, :ch] = jnp.zeros((out_ch, ch), BF16)
        for b in range(3):
            here = slice(b * ch, (b + 1) * ch)
            wf[a, here, :ch] = w_first[a, b]
            wf[a, here, ch:] = (w_first[a, b].astype(F32) * mask_first).astype(BF16)
            student = w_down[a, b].astype(F32) * mask_down
            wd[0, a, here] = w_down[a, b]
            wd[1, a, here] = student.astype(BF16)
            turned = student.T.astype(BF16)
            if b == 0:
                wt[a, out_ch:, ch:] = turned
            elif b == 1:
                wt[a, :out_ch, :ch] = turned
            else:
                wt[a, :out_ch, ch:] = turned
    ids = jnp.broadcast_to(group_ids[...].astype(F32), (ch, ch))
    member = (ids == ids.T).astype(F32)
    gain, bias = gain_ref[...], bias_ref[...]

    top = lax.broadcasted_iota(jnp.int32, (16, ch), 0) == 0
    foot = lax.broadcasted_iota(jnp.int32, (16, ch), 0) == 15
    tmp[...] = jnp.zeros(tmp.shape, F32)

    def spread_row(e, r, at):
        tmp[e, 16 : 16 + cols] = ext[at, 16 : 16 + cols].astype(F32)
        for k in range(4):
            taps[e, r, :, k * ch : (k + 1) * ch] = tmp[e, pl.ds(15 + k, wide, stride=2), :].astype(BF16)

    def mend_row(e, r, at):
        before = pltpu.roll(ext[at, :16].astype(F32), 1, 0)
        after = pltpu.roll(ext[at, 16 + cols :].astype(F32), 15, 0)
        head = taps[e, r, :16, :ch].astype(F32)
        tail = taps[e, r, wide - 16 :, 3 * ch :].astype(F32)
        taps[e, r, :16, :ch] = jnp.where(top, before, head).astype(BF16)
        taps[e, r, wide - 16 :, 3 * ch :] = jnp.where(foot, after, tail).astype(BF16)

    def spread(r, carry):
        spread_row(1, r, 2 * r + 1)
        spread_row(0, r + 1, 2 * r + 2)
        return carry

    def mend_field(r, carry):
        mend_row(0, r, 2 * r)
        mend_row(1, r, 2 * r + 1)
        return carry

    own.wait()
    lax.fori_loop(0, half, spread, 0)
    finish_receives(halos)
    spread_row(0, 0, 0)
    spread_row(1, half, rows + 1)
    lax.fori_loop(0, half + 1, mend_field, 0)

    size = BLOCK * wide
    total = jnp.zeros((1, 2 * ch), F32)
    for e in range(2):
        for p in range(2):

            def convolve(step, carry, e=e, p=p):
                r = step * BLOCK
                acc = None
                for a in range(3):
                    lhs = taps[(e + a) % 2, pl.ds(r + (e + a) // 2, BLOCK), :, p * ch : (p + 3) * ch]
                    part = dot(lhs.reshape(size, 3 * ch), wf[a])
                    acc = part if acc is None else acc + part
                pre[e, p, pl.ds(r, BLOCK)] = acc.reshape(BLOCK, wide, 2 * ch)
                return carry + jnp.sum(acc, axis=0, keepdims=True)

            total = lax.fori_loop(0, half // BLOCK, convolve, total)
    finish_sends(halos)

    def fold(value):
        return jnp.concatenate([value[:, :ch], value[:, ch:]], axis=0)

    cells = float(rows * cols)
    mean = total / cells

    def squares(r, carry):
        for e in range(2):
            for p in range(2):
                gap = pre[e, p, r] - mean
                carry = carry + jnp.sum(gap * gap, axis=0, keepdims=True)
        return carry

    spread_sum = lax.fori_loop(0, half, squares, jnp.zeros((1, 2 * ch), F32))

    def everyone(source, target, ssem, rsem):
        def start(k, carry):
            to = lax.rem(me + k, devices)
            remote(source(to), target.at[me], ssem.at[k], rsem.at[k], place(to)).start()
            return carry

        def receive(k, carry):
            at = lax.rem(me + devices - k, devices)
            remote(source(at), target.at[at], ssem.at[k], rsem.at[k], place(at)).wait_recv()
            return carry

        def sent(k, carry):
            to = lax.rem(me + k, devices)
            remote(source(to), target.at[me], ssem.at[k], rsem.at[k], place(to)).wait_send()
            return carry

        return (
            lambda: lax.fori_loop(1, devices, start, 0),
            lambda: lax.fori_loop(1, devices, receive, 0),
            lambda: lax.fori_loop(1, devices, sent, 0),
        )

    def grouped(value):
        return jnp.dot(value, member, precision=HIGH, preferred_element_type=F32)

    per_group = ch // GROUPS
    count = cells * devices * per_group
    stat_a[me] = jnp.concatenate([fold(mean), fold(spread_sum), jnp.zeros((4, ch), F32)], axis=0)
    go, receive, sent_a = everyone(lambda to: stat_a.at[me], stat_a, sa_s, sa_r)
    go()
    receive()
    stats = stat_a[...]
    centre8 = grouped(jnp.sum(stats, axis=0)) / float(devices * per_group)
    centre2 = centre8[0:2]
    drift = stats[:, 0:2] - centre2[None]
    moment = jnp.sum(stats[:, 2:4] + cells * (drift * drift), axis=0)
    variance = grouped(jnp.concatenate([moment, jnp.zeros((6, ch), F32)], axis=0))[0:2] / count
    inv2 = lax.rsqrt(variance + EPS)
    centre_s, inv_s = centre2[1:2], inv2[1:2]
    centre_both = jnp.concatenate([centre2[0:1], centre_s], axis=1)
    inv_both = jnp.concatenate([inv2[0:1], inv_s], axis=1)
    gain_both = jnp.concatenate([gain, gain], axis=1)
    bias_both = jnp.concatenate([bias, bias], axis=1)

    crest = lax.broadcasted_iota(jnp.int32, (wide, 2 * ch), 0) == 0

    def activate(r, carry):
        for e in range(2):
            at = r + 1 if e else r + half + 1
            for p in range(2):
                normed = (pre[e, p, r] - centre_both) * inv_both * gain_both + bias_both
                value = normed * jax.nn.sigmoid(normed)
                rounded = value.astype(BF16)
                for net in range(2):
                    hid[net, at, :, (p + 1) * ch : (p + 2) * ch] = rounded[:, net * ch : (net + 1) * ch]
                if p:
                    value = rounded.astype(F32)
                    hcol[pl.ds(e * half + r, 1), :] = value[wide - 1 :, :]
                    rolled = jnp.where(crest, 0.0, pltpu.roll(value, 1, 0)).astype(BF16)
                    for net in range(2):
                        hid[net, at, :, :ch] = rolled[:, net * ch : (net + 1) * ch]
        return carry

    lax.fori_loop(0, half, activate, 0)
    hids = [
        (remote(hid.at[:, half], hrow_in, hid_s.at[0], hid_r.at[0], (down, lon)), has_down, has_up),
        (remote(hcol, hcol_in, hid_s.at[1], hid_r.at[1], (lat, east)), None, None),
        (remote(hcol.at[pl.ds(rows - 8, 8)], hcorner, hid_s.at[2], hid_r.at[2], (down, east)), has_down, has_up),
    ]
    begin(hids)
    sent_a()

    @pl.when(jnp.logical_not(has_up))
    def _():
        hrow_in[...] = jnp.zeros(hrow_in.shape, BF16)
        hcorner[...] = jnp.zeros(hcorner.shape, F32)

    hid[:, 0] = jnp.zeros((2, wide, 3 * ch), BF16)
    starts = (0, half + 1, 1)
    scale = LOSS_WEIGHT / float(half * wide * devices)

    def shrink(step, carry):
        r = step * BLOCK
        for net in range(2):
            acc = None
            for a in range(3):
                lhs = hid[net, pl.ds(r + starts[a], BLOCK)].reshape(size, 3 * ch)
                part = dot(lhs, wd[net, a])
                acc = part if acc is None else acc + part
            outs[net, pl.ds(r, BLOCK)] = acc.reshape(BLOCK, wide, out_ch)
        return carry

    lax.fori_loop(0, half // BLOCK, shrink, 0)
    finish_sends(hids)
    finish_receives(hids)
    west_even, west_odd = hcol_in[:half, :], hcol_in[half:, :]
    west_last = jnp.concatenate([hcorner[7:8, :], west_odd[: half - 1]], axis=0)
    for net in range(2):
        here = slice(net * ch, (net + 1) * ch)
        acc = dot(hrow_in[net], wd[net, 0])
        outs[net, 0] = outs[net, 0] + acc
        acc = None
        for a, value in enumerate((west_last, west_even, west_odd)):
            part = dot(value[:, here].astype(BF16), wd[net, a, :ch])
            acc = part if acc is None else acc + part
        edge[net] = acc
    start_col = lax.broadcasted_iota(jnp.int32, (wide, out_ch), 0) == 0

    def finish_row(r, carry):
        both = []
        for net in range(2):
            extra = jnp.broadcast_to(edge[net, pl.ds(r, 1), :], (wide, out_ch))
            both.append(outs[net, r] + jnp.where(start_col, extra, 0.0))
        out_ref[r] = both[1].astype(BF16)
        ct = (scale * (both[1] - both[0])).astype(BF16)
        cot[r, :, :out_ch] = ct
        line = ct.astype(F32)
        ccol[pl.ds(r, 1), :] = line[0:1]
        cot[r, :, out_ch:] = pltpu.roll(line, wide - 1, 0).astype(BF16)
        return carry

    lax.fori_loop(0, half, finish_row, 0)
    cots = [
        (remote(cot.at[0], cot.at[half], cot_s.at[0], cot_r.at[0], (up, lon)), has_up, has_down),
        (remote(ccol, ccol_in, cot_s.at[1], cot_r.at[1], (lat, west)), None, None),
        (remote(ccol.at[pl.ds(0, 8)], ccorner, cot_s.at[2], cot_r.at[2], (up, west)), has_up, has_down),
    ]
    begin(cots)

    @pl.when(jnp.logical_not(has_down))
    def _():
        cot[half] = jnp.zeros((wide, 2 * out_ch), BF16)
        ccorner[...] = jnp.zeros(ccorner.shape, F32)

    for step in range(half // BLOCK):
        piece = cot[step * BLOCK : (step + 1) * BLOCK, :, :out_ch].reshape(size, out_ch)
        cturn[:, step * size : (step + 1) * size] = piece.astype(F32).T.astype(BF16)
    def put_west(at, value):
        tile = hid[1, at, :16, :ch].astype(F32)
        new = jnp.broadcast_to(value[:, ch:], (16, ch))
        hid[1, at, :16, :ch] = jnp.where(top, new, tile).astype(BF16)

    def mend(r, carry):
        put_west(r + half + 1, hcol_in[pl.ds(r, 1), :])
        put_west(r + 1, hcol_in[pl.ds(r + half, 1), :])
        return carry

    hid[1, 0] = hrow_in[1]
    lax.fori_loop(0, half, mend, 0)
    put_west(0, hcorner[7:8, :])
    gd[9 * ch :, :] = jnp.zeros((16, out_ch), F32)
    gf[9 * ch :, :] = jnp.zeros((16, ch), F32)
    for a in range(3):
        turned = dot(cturn[...], hid[1, starts[a] : starts[a] + half].reshape(half * wide, 3 * ch))
        for b in range(3):
            at = (a * 3 + b) * ch
            gd[at : at + ch, :] = turned[:, b * ch : (b + 1) * ch].T * mask_down
    pairs = devices // 2
    core = lax.rem(lon, 2)
    mine = me // 2
    mate = (lat, lon + 1 - 2 * core)

    def pack(grads, buffer):
        for d in range(devices):
            buffer[d % 2, d // 2] = grads[d * chunk : d * chunk + padded, :].astype(BF16)

    def merge(buffer, other, merged, got):
        def one_chunk(h, carry):
            merged[h] = (buffer[core, h].astype(F32) + other[h].astype(F32)).astype(BF16)
            return carry

        lax.fori_loop(0, pairs, one_chunk, 0)
        got[mine] = merged[mine]

    def scatter(merged, got, ssem, rsem):
        def owner(h):
            return place(2 * h + core)

        def start(k, carry):
            to = lax.rem(mine + k, pairs)
            remote(merged.at[to], got.at[mine], ssem.at[k], rsem.at[k], owner(to)).start()
            return carry

        def receive(k, carry):
            at = lax.rem(mine + pairs - k, pairs)
            remote(merged.at[at], got.at[at], ssem.at[k], rsem.at[k], owner(at)).wait_recv()
            return carry

        def sent(k, carry):
            to = lax.rem(mine + k, pairs)
            remote(merged.at[to], got.at[mine], ssem.at[k], rsem.at[k], owner(to)).wait_send()
            return carry

        return (
            lambda: lax.fori_loop(1, pairs, start, 0),
            lambda: lax.fori_loop(1, pairs, receive, 0),
            lambda: lax.fori_loop(1, pairs, sent, 0),
        )

    pack(gd, send_d)
    swap_d = remote(send_d.at[1 - core], other_d, swap_s.at[0], swap_r.at[0], mate)
    swap_d.start()
    finish_sends(cots)
    finish_receives(cots)
    bottom = lax.broadcasted_iota(jnp.int32, (16, out_ch), 0) == 15

    def put_east(at, value):
        tile = cot[at, wide - 16 :, out_ch:].astype(F32)
        cot[at, wide - 16 :, out_ch:] = jnp.where(bottom, jnp.broadcast_to(value, (16, out_ch)), tile).astype(BF16)

    def mend_east(r, carry):
        put_east(r, ccol_in[pl.ds(r, 1), :])
        return carry

    lax.fori_loop(0, half, mend_east, 0)
    put_east(half, ccorner[0:1, :])

    def backward(step, carry):
        r = step * BLOCK
        here = cot[pl.ds(r, BLOCK)].reshape(size, 2 * out_ch)
        after = cot[pl.ds(r + 1, BLOCK)].reshape(size, 2 * out_ch)
        pair = (dot(here, wt[1]), dot(here, wt[2]) + dot(after, wt[0]))
        one, two = carry
        for e in range(2):
            for p in range(2):
                hat = (pre[e, p, pl.ds(r, BLOCK), :, ch:].reshape(size, ch) - centre_s) * inv_s
                normed = hat * gain + bias
                sigma = jax.nn.sigmoid(normed)
                value = pair[e][:, p * ch : (p + 1) * ch] * sigma * (1.0 + normed * (1.0 - sigma)) * gain
                ghat[e, pl.ds(r, BLOCK), :, p * ch : (p + 1) * ch] = value.reshape(BLOCK, wide, ch)
                one = one + jnp.sum(value, axis=0, keepdims=True)
                two = two + jnp.sum(value * hat, axis=0, keepdims=True)
        return one, two

    zero = jnp.zeros((1, ch), F32)
    one, two = lax.fori_loop(0, half // BLOCK, backward, (zero, zero))
    stat_b[me] = jnp.concatenate([one, two, jnp.zeros((6, ch), F32)], axis=0)
    go, receive_b, sent_b = everyone(lambda to: stat_b.at[me], stat_b, sb_s, sb_r)
    go()

    go_d, receive_d, sent_d = scatter(merged_d, got_d, rd_s, rd_r)

    swap_d.wait_recv()
    merge(send_d, other_d, merged_d, got_d)
    go_d()
    receive_b()
    back = grouped(jnp.sum(stat_b[...], axis=0)) / count
    m1, m2 = back[0:1], back[1:2]
    for e in range(2):
        for step in range(half // BLOCK):
            r = step * BLOCK
            for p in range(2):
                hat = (pre[e, p, r : r + BLOCK, :, ch:].reshape(size, ch) - centre_s) * inv_s
                value = ghat[e, r : r + BLOCK, :, p * ch : (p + 1) * ch].reshape(size, ch)
                gpre = inv_s * (value - m1 - hat * m2)
                gturn[e, p * ch : (p + 1) * ch, step * size : (step + 1) * size] = gpre.T.astype(BF16)
    for a in range(3):
        acc = None
        for e in range(2):
            start = (e + a) // 2
            part = dot(gturn[e], taps[(e + a) % 2, start : start + half].reshape(half * wide, 4 * ch))
            acc = part if acc is None else acc + part
        for b in range(3):
            at = (a * 3 + b) * ch
            block = acc[:ch, b * ch : (b + 1) * ch] + acc[ch:, (b + 1) * ch : (b + 2) * ch]
            gf[at : at + ch, :] = block.T * mask_first
    pack(gf, send_f)
    swap_f = remote(send_f.at[1 - core], other_f, swap_s.at[1], swap_r.at[1], mate)
    swap_f.start()
    go_f, receive_f, sent_f = scatter(merged_f, got_f, rf_s, rf_r)

    def add_up(got, width):
        def add(d, acc):
            return acc + got[d].astype(F32)

        return lax.fori_loop(0, pairs, add, jnp.zeros((padded, width), F32))[:chunk]

    receive_d()
    gdown_ref[...] = add_up(got_d, out_ch)
    swap_f.wait_recv()
    merge(send_f, other_f, merged_f, got_f)
    go_f()
    receive_f()
    gfirst_ref[...] = add_up(got_f, ch)
    sent_b()
    sent_d()
    sent_f()
    swap_d.wait_send()
    swap_f.wait_send()


def local(nlat, nlon, field, w_first, w_down, keep_first, chan_first, keep_down, chan_down, group_ids, norm_gain, norm_bias):
    rows, cols, ch = field.shape
    out_ch = w_down.shape[3]
    devices = nlat * nlon
    pairs = devices // 2
    half, wide = rows // 2, cols // 2
    chunk = 9 * ch // devices
    padded = -(-chunk // 16) * 16
    vmem = pl.BlockSpec(memory_space=pltpu.VMEM)
    dma = pltpu.SemaphoreType.DMA
    S = pltpu.VMEM
    return tuple(
        pl.pallas_call(
            functools.partial(kernel, nlat, nlon, chunk, padded),
            out_shape=(
                jax.ShapeDtypeStruct((half, wide, out_ch), BF16),
                jax.ShapeDtypeStruct((chunk, ch), F32),
                jax.ShapeDtypeStruct((chunk, out_ch), F32),
            ),
            in_specs=[pl.BlockSpec(memory_space=pl.ANY)] + [vmem] * 9,
            out_specs=(vmem, vmem, vmem),
            scratch_shapes=[
                S((rows + 2, cols + 32, ch), BF16),
                S((2, cols + 32, ch), F32),
                S((2, half + 1, wide, 4 * ch), BF16),
                S((2, 2, half, wide, 2 * ch), F32),
                S((2, rows + 1, wide, 3 * ch), BF16),
                S((rows, 2 * ch), F32),
                S((rows, 2 * ch), F32),
                S((8, 2 * ch), F32),
                S((2, wide, 3 * ch), BF16),
                S((2, half, wide, out_ch), F32),
                S((2, half, out_ch), F32),
                S((half + 1, wide, 2 * out_ch), BF16),
                S((half, out_ch), F32),
                S((half, out_ch), F32),
                S((8, out_ch), F32),
                S((2, half, wide, 2 * ch), F32),
                S((2, 2 * ch, half * wide), BF16),
                S((out_ch, half * wide), BF16),
                S((3, 3 * ch, 2 * ch), BF16),
                S((2, 3, 3 * ch, out_ch), BF16),
                S((3, 2 * out_ch, 2 * ch), BF16),
                S((9 * ch + 16, ch), F32),
                S((9 * ch + 16, out_ch), F32),
                S((2, pairs, padded, ch), BF16),
                S((2, pairs, padded, out_ch), BF16),
                S((pairs, padded, ch), BF16),
                S((pairs, padded, out_ch), BF16),
                S((pairs, padded, ch), BF16),
                S((pairs, padded, out_ch), BF16),
                S((pairs, padded, ch), BF16),
                S((pairs, padded, out_ch), BF16),
                S((devices, 8, ch), F32),
                S((devices, 8, ch), F32),
                dma,
                dma((8,)), dma((8,)),
                dma((3,)), dma((3,)),
                dma((3,)), dma((3,)),
                dma((devices,)), dma((devices,)),
                dma((devices,)), dma((devices,)),
                dma((2,)), dma((2,)),
                dma((pairs,)), dma((pairs,)),
                dma((pairs,)), dma((pairs,)),
            ],
            compiler_params=pltpu.CompilerParams(
                collective_id=0, has_side_effects=True, vmem_limit_bytes=56 * 1024 * 1024
            ),
        )(
            field,
            w_first,
            w_down,
            keep_first,
            chan_first.reshape(1, ch),
            keep_down,
            chan_down.reshape(1, out_ch),
            group_ids.reshape(1, ch),
            norm_gain.reshape(1, ch),
            norm_bias.reshape(1, ch),
        )
    )


def solution(mesh):
    return jax.shard_map(
        functools.partial(local, mesh.shape["lat"], mesh.shape["lon"]),
        mesh=mesh,
        in_specs=(P("lat", "lon", None), P(), P(), P(), P(), P(), P(), P(), P(), P()),
        out_specs=(P("lat", "lon", None), P(("lat", "lon"), None), P(("lat", "lon"), None)),
        check_vma=False,
    )
```
